256 devices in a mesh: scan: 128 (over y, z, x), det: 2 (over core).
Axes of the slice: x: 4, y: 4, z: 8, core: 2. Of those that a mesh axis runs over, the one named last changes fastest.
Arguments:
- frames: float32 [256, 512, 512], P('det', 'scan'), may hold values from -6 to 6
- aperture: int32 [256], replicated, may hold values 0 or 1
- upper_pixels: int32 [128, 64], replicated, may hold values from -1 to 255, as said below
- lower_pixels: int32 [128, 64], replicated, may hold values from -1 to 255, as said below
Outputs:
- spectrum: float32 [2, 512, 512], P(None, 'scan', 'det')
- object_wave: float32 [2, 512, 512], P(None, 'det', 'scan')
The draws below stay inside these ranges and needn't reach their ends.
Inputs may be any that keep to these rules, and one draw needn't show every extreme that they name: `upper_pixels`: each row lists pixels of one frequency block: 1 to 64 pixel numbers, then -1 to the end of the row; some row is full and some row has a single entry. A pixel may appear more than once. `lower_pixels`: as for upper_pixels.
All inputs are finite; a program needn't handle non-finite values.
Results may differ from the reference program's by a relative error of at most 0.0001.
Values sent between devices are 32-bit elements; how exact they have to be, the bound alone decides.
A program may use at most 192 MiB of HBM per device.

```python
import jax
import jax.numpy as jnp
from jax import lax

SCAN = 512
LIST = 64
PIXELS = 256
BLOCKS = 128


def pixel_list(key):
    key_len, key_full, key_ids = jax.random.split(key, 3)
    lengths = jax.random.randint(key_len, (BLOCKS,), 1, LIST + 1)
    full_block = jax.random.randint(key_full, (), 0, BLOCKS)
    block_ids = jnp.arange(BLOCKS, dtype=jnp.int32)
    lengths = jnp.where(block_ids == full_block, LIST, lengths)
    lengths = jnp.where(block_ids == (full_block + 1) % BLOCKS, 1, lengths)
    pixel_ids = jax.random.randint(key_ids, (BLOCKS, LIST), 0, PIXELS)
    first_entry = (block_ids[:, None] == full_block) & (jnp.arange(LIST, dtype=jnp.int32)[None, :] == 0)
    pixel_ids = jnp.where(first_entry, PIXELS - 1, pixel_ids)
    listed = jnp.arange(LIST, dtype=jnp.int32)[None, :] < lengths[:, None]
    return jnp.where(listed, pixel_ids, -1).astype(jnp.int32)


def draw_upper_pixels(key, part):
    key = jax.random.fold_in(key, 11)
    return pixel_list(key)


def draw_lower_pixels(key, part):
    key = jax.random.fold_in(key, 23)
    return pixel_list(key)


def set_ends(entries, stream_key, smallest, top_value):
    longest = entries.shape.index(max(entries.shape))
    spots = []
    for shift in (0, 1):
        where = [jax.random.randint(jax.random.fold_in(stream_key, axis), (), 0, length) for axis, length in enumerate(entries.shape)]
        where[longest] = (where[longest] + shift) % entries.shape[longest]
        spots.append(tuple(where))
    return entries.at[spots[0]].set(smallest).at[spots[1]].set(top_value)


def shard_levels(stream_key, dims, cuts, least, high):
    factor_of, own = 1.0, jax.random.fold_in(stream_key, 6)
    for axis_at, blocks in cuts:
        draws = jnp.exp(jax.random.uniform(jax.random.fold_in(own, axis_at), (blocks,), jnp.float32, least / len(cuts), high / len(cuts)))
        factor_of = factor_of * jnp.repeat(draws, dims[axis_at] // blocks).reshape([-1 if axis == axis_at else 1 for axis in range(len(dims))])
    return factor_of


def centred(stream_key, extent, deviation, most, pieces=(), held_as=jnp.bfloat16):
    drawn = deviation * jax.random.normal(stream_key, extent, jnp.float32)
    if pieces:
        drawn = drawn * shard_levels(stream_key, extent, pieces, -0.22, 0.18)
    return jnp.clip(drawn, -most, most).astype(held_as)


def setup_inputs(seed: int = 0) -> dict:
    keys = jax.random.split(jax.random.key(seed), 5)
    return {
        "frames": centred(keys[0], (PIXELS, SCAN, SCAN), 1.0, 6.0, ((0, 2), (1, 128)), jnp.float32),
        "aperture": set_ends((jax.random.randint(keys[1], (PIXELS,), 0, 4) < 3).astype(jnp.int32), jax.random.fold_in(keys[1], 1), 0, 1),
        "upper_pixels": draw_upper_pixels(jax.random.fold_in(keys[4], 71), 0),
        "lower_pixels": draw_lower_pixels(jax.random.fold_in(keys[4], 71), 0),
    }


def intersection_weight(aperture, upper_pixels, lower_pixels):
    pixel_ids = jnp.arange(PIXELS, dtype=jnp.int32)
    upper_hits = jnp.sum((upper_pixels[:, :, None] == pixel_ids[None, None, :]).astype(jnp.int32), axis=1)
    lower_hits = jnp.sum((lower_pixels[:, :, None] == pixel_ids[None, None, :]).astype(jnp.int32), axis=1)
    counts = upper_hits - lower_hits
    return (counts * aperture[None, :]).astype(jnp.float32) * (LIST ** -0.5)


def reference(frames, aperture, upper_pixels, lower_pixels):
    weight = intersection_weight(aperture, upper_pixels, lower_pixels)
    row_weight = jnp.repeat(weight, SCAN // BLOCKS, axis=0)
    groups = PIXELS // 16
    grouped_frames = frames.reshape(groups, 16, SCAN, SCAN)
    grouped_weight = row_weight.reshape(SCAN, groups, 16).transpose(1, 0, 2)

    def accumulate(carry, inputs):
        frame_group, weight_group = inputs
        transformed = jnp.fft.fft2(frame_group, norm="ortho")
        real_part = jnp.einsum("kqp,qk->qp", transformed.real, weight_group, precision=lax.Precision.HIGHEST)
        imag_part = jnp.einsum("kqp,qk->qp", transformed.imag, weight_group, precision=lax.Precision.HIGHEST)
        return (carry[0] + real_part, carry[1] + imag_part), None

    zeros_field = jnp.zeros((SCAN, SCAN), jnp.float32)
    (spec_real, spec_imag), unused = lax.scan(accumulate, (zeros_field, zeros_field), (grouped_frames, grouped_weight))
    spectrum = jnp.stack((spec_real, spec_imag))
    wave = jnp.fft.ifft2(spec_real + 1j * spec_imag, norm="ortho")
    object_wave = jnp.stack((wave.real, wave.imag)).astype(spectrum.dtype)
    return spectrum, object_wave
```

```python
import math

import jax
import jax.numpy as jnp
from jax import lax
from jax.experimental import pallas as pl
from jax.experimental.pallas import tpu as pltpu
from jax.sharding import PartitionSpec as P

MESH = pl.DeviceIdType.MESH
F32 = jnp.float32
BF16 = jnp.bfloat16
UNIT = 2.0 * math.pi / 512
SIN = (-1.0 / 6, 1.0 / 120, -1.0 / 5040, 1.0 / 362880, -1.0 / 39916800)


def cos512(m):
    m = m & 511
    t = (128 - jnp.minimum(m, 512 - m)).astype(F32) * UNIT
    t2 = t * t
    poly = jnp.full_like(t, SIN[-1])
    for coefficient in SIN[-2::-1]:
        poly = poly * t2 + coefficient
    return t + t * (t2 * poly)


def split(a):
    high = a.astype(BF16)
    return high, (a - high.astype(F32)).astype(BF16)


def dot(a, b):
    return jnp.dot(a, b, preferred_element_type=F32)


def dot3(a, b_high, b_low):
    rows = a.shape[0]
    a_high, a_low = split(a)
    both = dot(jnp.concatenate((a_high, a_low), axis=0), b_high)
    return both[:rows] + both[rows:] + dot(a_high, b_low)


def iota(shape, dimension):
    return lax.broadcasted_iota(jnp.int32, shape, dimension)


def kernel(
    frames, aperture, upper, lower,
    spectrum, wave,
    f, ap, up, lo, w_lo, w_hi,
    a, r1, t1, r2, t2, r3, t3, r_pair, turned, pm, r4, q, r5, e_high, e_low,
    load_sem, pair_sem, sem1, sem2, sem3, sem4, send5, recv5,
):
    s = lax.axis_index("scan")
    c = lax.axis_index("det")
    y, z, x = s // 32, (s // 4) % 8, s % 4
    u, v = x * (1 - c) + y * c, y * (1 - c) + x * c
    su, sv = 1 - c + 32 * c, 32 * (1 - c) + c

    loads = [
        pltpu.make_async_copy(upper, up, load_sem.at[0]),
        pltpu.make_async_copy(lower, lo, load_sem.at[1]),
        pltpu.make_async_copy(aperture, ap, load_sem.at[2]),
        pltpu.make_async_copy(frames.at[:, c], f.at[pl.ds(c * 128, 128)], load_sem.at[3]),
    ]
    for load in loads:
        load.start()

    def u_peer(d):
        return s + ((u + d) % 4 - u) * su

    def v_peer(d):
        return s + ((v + d) % 4 - v) * sv

    def z_peer(d):
        return s + ((z + d) % 8 - z) * 4

    barrier = pltpu.get_barrier_semaphore()

    def greet(scan, det):
        pl.semaphore_signal(barrier, inc=1, device_id=(scan, det), device_id_type=MESH)

    greet(s, 1 - c)
    for d in range(1, 4):
        greet(u_peer(d), c)
        greet(v_peer(d), c)
    for d in range(1, 8):
        greet(z_peer(d), c)
    source_core = y // 2
    for i in range(16):
        chip = (i // 4) * 32 + z * 4 + i % 4

        @pl.when(jnp.logical_or(chip != s, source_core != c))
        def _():
            greet(chip, source_core)

    own = jnp.where(source_core == c, 1, 0)
    pl.semaphore_wait(barrier, 30 - own)

    swap = pltpu.make_async_remote_copy(
        src_ref=frames.at[:, 1 - c], dst_ref=f.at[pl.ds(c * 128, 128)],
        send_sem=pair_sem.at[0], recv_sem=pair_sem.at[1], device_id=(s, 1 - c), device_id_type=MESH,
    )
    swap.start()

    for load in loads[:3]:
        load.wait()
    pixel = iota((256, 128), 0)

    def count(j, total):
        plus = jnp.where(up[pl.ds(j, 1), :] == pixel, 1, 0)
        return total + plus - jnp.where(lo[pl.ds(j, 1), :] == pixel, 1, 0)

    counts = lax.fori_loop(0, 64, count, jnp.zeros((256, 128), jnp.int32))
    scaled = counts.astype(F32) * (64**-0.5 / 512)
    w_lo[...] = scaled[:128].T
    w_hi[...] = scaled[128:].T
    inside = ap[...].astype(F32)
    tiles = []
    for i in range(16):
        start = (i // 4) * su + (i % 4) * sv
        rows = pl.ds(start, 8, stride=4)
        tiles.append(jnp.concatenate((w_lo[rows, :], w_hi[rows, :]), axis=1))
    weight = (jnp.concatenate(tiles, axis=0) * inside).astype(BF16)

    loads[3].wait()
    swap.wait_recv()
    flat = f.reshape(2048, 128)
    for i in range(4):
        part = jnp.concatenate([flat[pl.ds(4 * j + i, 256, stride=8), :] for j in range(2)], axis=1)
        high, low = split(part)
        total = dot(weight, high) + dot(weight, low)
        a[:, :, i] = total.reshape(4, 4, 8, 256)

    first = []
    for d in range(1, 4):
        first.append(pltpu.make_async_remote_copy(
            src_ref=a.at[(u + d) % 4], dst_ref=r1.at[d - 1], send_sem=sem1.at[0, d - 1], recv_sem=sem1.at[1, d - 1],
            device_id=(u_peer(d), c), device_id_type=MESH,
        ))
    for copy in first:
        copy.start()

    frequency = iota((256, 512), 1)
    wide = frequency % 256 + 256 * c
    table = cos512(wide * iota((256, 512), 0) - 128 * (frequency // 256))
    table_high, table_low = split(table)
    e_high[...] = table_high
    e_low[...] = table_low

    row, column = iota((64, 128), 0), iota((64, 128), 1)
    rho = row % 8
    place = 4 * (((u - column // 32) & 3) * su + v * sv + 4 * z) + (column // 8) % 4
    same = (row // 8) == (column % 8)
    lefts = []
    for d in range(4):
        block = u * su + ((v + d) % 4) * sv + 4 * (row // 8)
        left = cos512((4 * block + rho % 4) * place + 128 * (rho // 4))
        lefts.append(split(jnp.where(same, left, 0.0)))

    for copy in first:
        copy.wait_recv()

    second = []
    for d in (1, 2, 3, 0):
        vb = (v + d) % 4
        rows = [a[u, vb].reshape(32, 256)] + [r1[j, vb].reshape(32, 256) for j in range(3)]
        right_high, right_low = split(jnp.concatenate(rows, axis=0))
        left_high, left_low = lefts[d]
        both = dot(jnp.concatenate((left_high, left_low), axis=0), right_high)
        t1[d] = both[:64] + both[64:] + dot(left_high, right_low)
        if d:
            copy = pltpu.make_async_remote_copy(
                src_ref=t1.at[d], dst_ref=r2.at[d - 1], send_sem=sem2.at[0, d - 1], recv_sem=sem2.at[1, d - 1],
                device_id=(v_peer(d), c), device_id_type=MESH,
            )
            copy.start()
            second.append(copy)
    for copy in second:
        copy.wait_recv()
    t2[...] = (t1[0] + r2[0] + r2[1] + r2[2]).reshape(8, 8, 256)

    third = []
    for d in range(1, 8):
        copy = pltpu.make_async_remote_copy(
            src_ref=t2.at[(z + d) % 8], dst_ref=r3.at[d - 1], send_sem=sem3.at[0, d - 1], recv_sem=sem3.at[1, d - 1],
            device_id=(z_peer(d), c), device_id_type=MESH,
        )
        copy.start()
        third.append(copy)
    n = iota((128, 256), 1)
    source = iota((128, 256), 0)
    source_block = (source // 32) * 32 + (source // 8) % 4 + 4 * ((z - source % 8) & 7)
    back_high, back_low = split(cos512(4 * source_block * (n % 128) - 128 * (n // 128)))
    for copy in third:
        copy.wait_recv()
    total = t2[z]
    for d in range(7):
        total = total + r3[d]
    t3[...] = total

    other = pltpu.make_async_remote_copy(
        src_ref=t3, dst_ref=r_pair, send_sem=pair_sem.at[2], recv_sem=pair_sem.at[3],
        device_id=(s, 1 - c), device_id_type=MESH,
    )
    other.start()

    lane = iota((32, 128), 1)
    for half in range(2):
        tile = total[:, half * 128 : (half + 1) * 128]
        turned[...] = jnp.concatenate([tile] * 16, axis=0).T
        packed = jnp.zeros((32, 128), F32)
        for i in range(4):
            packed = jnp.where(lane // 8 == i, turned[pl.ds(i, 32, stride=4), :], packed)
        for i in range(8):
            pm[i, half * 4 : half * 4 + 4, :] = packed[i * 4 : i * 4 + 4]
    fourth = []
    for d in range(1, 8):
        copy = pltpu.make_async_remote_copy(
            src_ref=pm.at[(z + d) % 8], dst_ref=r4.at[d], send_sem=sem4.at[0, d - 1], recv_sem=sem4.at[1, d - 1],
            device_id=(z_peer(d), c), device_id_type=MESH,
        )
        copy.start()
        fourth.append(copy)
    r4[0] = pm[z]
    for copy in fourth:
        copy.wait_recv()

    flat4 = r4.reshape(64, 128)
    me = y * 4 + x
    for i in range(8):
        q[i] = flat4[pl.ds(i, 8, stride=8), :]

    def out_copy(i, core, chip):
        return pltpu.make_async_remote_copy(
            src_ref=q.at[i], dst_ref=r5.at[me], send_sem=send5.at[2 * i + core], recv_sem=recv5.at[me],
            device_id=(chip, core), device_id_type=MESH,
        )

    for i in range(8):
        chip = (2 * c + i // 4) * 32 + z * 4 + i % 4
        for core in range(2):
            mine = jnp.logical_and(chip == s, c == core)

            @pl.when(jnp.logical_not(mine))
            def _():
                out_copy(i, core, chip).start()

            @pl.when(mine)
            def _():
                pltpu.make_async_copy(q.at[i], r5.at[me], recv5.at[me]).start()

    other.wait_recv()
    sums = dot3(jnp.concatenate((total, r_pair[...]), axis=0), e_high[...], e_low[...])
    lane = iota((8, 256), 1)
    sign = (1 - 2 * (lane % 2)).astype(F32)
    near, far = jnp.where(c == 0, 1.0, sign), jnp.where(c == 0, sign, 1.0)
    cosine = near * sums[:8, :256] + far * sums[8:, :256]
    sine = near * sums[:8, 256:] + far * sums[8:, 256:]
    side = jnp.where(iota((8, 256), 0) < 4, -1.0, 1.0)
    result = cosine - side * jnp.concatenate((sine[4:], sine[:4]), axis=0)
    spectrum[0] = result[:4]
    spectrum[1] = result[4:]

    rho = iota((8, 256), 0)
    angle = (rho % 4) * (lane + 256 * c) + 128 * (rho // 4)
    turn_real, turn_imag = cos512(angle), cos512(angle - 128)

    for i in range(16):
        pltpu.make_async_copy(q.at[0], r5.at[i], recv5.at[i]).wait()
    right = r5.reshape(128, 128)[...].T[:32]
    moved = dot3(right, back_high, back_low)
    reals, imags = [], []
    for i in range(4):
        tile = moved[8 * i : 8 * i + 8]
        sine = tile[:, 128:]
        pair = tile[:, :128] + side[:, :128] * jnp.concatenate((sine[4:], sine[:4]), axis=0)
        twice = jnp.concatenate((pair, pair), axis=1)
        reals.append(jnp.sum(twice * turn_real, axis=0, keepdims=True))
        imags.append(jnp.sum(twice * turn_imag, axis=0, keepdims=True))
    wave[0] = jnp.concatenate(reals, axis=0)
    wave[1] = jnp.concatenate(imags, axis=0)

    swap.wait_send()
    other.wait_send()
    for copy in first + second + third + fourth:
        copy.wait_send()
    for i in range(8):
        chip = (2 * c + i // 4) * 32 + z * 4 + i % 4
        for core in range(2):

            @pl.when(jnp.logical_or(chip != s, c != core))
            def _():
                out_copy(i, core, chip).wait_send()


def per_device(frames, aperture, upper_pixels, lower_pixels):
    tiled = frames.reshape(128, 4, 4, 128).transpose(0, 2, 1, 3).reshape(128, 2, 8, 128)
    anywhere = pl.BlockSpec(memory_space=pl.ANY)
    vmem = pl.BlockSpec(memory_space=pltpu.VMEM)
    dma = pltpu.SemaphoreType.DMA
    spectrum, wave = pl.pallas_call(
        kernel,
        out_shape=(jax.ShapeDtypeStruct((2, 4, 256), F32), jax.ShapeDtypeStruct((2, 4, 256), F32)),
        in_specs=[anywhere] * 4,
        out_specs=(vmem, vmem),
        scratch_shapes=[
            pltpu.VMEM((256, 8, 128), F32),
            pltpu.VMEM((1, 256), jnp.int32),
            pltpu.VMEM((64, 128), jnp.int32),
            pltpu.VMEM((64, 128), jnp.int32),
            pltpu.VMEM((128, 128), F32),
            pltpu.VMEM((128, 128), F32),
            pltpu.VMEM((4, 4, 4, 8, 256), F32),
            pltpu.VMEM((3, 4, 4, 8, 256), F32),
            pltpu.VMEM((4, 64, 256), F32),
            pltpu.VMEM((3, 64, 256), F32),
            pltpu.VMEM((8, 8, 256), F32),
            pltpu.VMEM((7, 8, 256), F32),
            pltpu.VMEM((8, 256), F32),
            pltpu.VMEM((8, 256), F32),
            pltpu.VMEM((128, 128), F32),
            pltpu.VMEM((8, 8, 128), F32),
            pltpu.VMEM((8, 8, 128), F32),
            pltpu.VMEM((8, 8, 128), F32),
            pltpu.VMEM((16, 8, 128), F32),
            pltpu.VMEM((256, 512), BF16),
            pltpu.VMEM((256, 512), BF16),
            dma((4,)), dma((4,)), dma((2, 3)), dma((2, 3)), dma((2, 7)), dma((2, 7)), dma((16,)), dma((16,)),
        ],
        compiler_params=pltpu.CompilerParams(
            collective_id=0, has_side_effects=True, vmem_limit_bytes=32 * 1024 * 1024
        ),
    )(tiled, aperture.reshape(1, 256), upper_pixels.T, lower_pixels.T)
    return spectrum, wave.transpose(0, 2, 1)


def solution(mesh):
    placed = (P("det", "scan", None), P(), P(), P())
    return jax.shard_map(
        per_device,
        mesh=mesh,
        in_specs=placed,
        out_specs=(P(None, "scan", "det"), P(None, "det", "scan")),
        check_vma=False,
    )
```

```python
import math

import jax
import jax.numpy as jnp
from jax import lax
from jax.experimental import pallas as pl
from jax.experimental.pallas import tpu as pltpu
from jax.sharding import PartitionSpec as P

MESH = pl.DeviceIdType.MESH
F32 = jnp.float32
BF16 = jnp.bfloat16
UNIT = 2.0 * math.pi / 512
SIN = (-1.0 / 6, 1.0 / 120, -1.0 / 5040, 1.0 / 362880, -1.0 / 39916800)


def cos512(m):
    m = m & 511
    t = (128 - jnp.minimum(m, 512 - m)).astype(F32) * UNIT
    t2 = t * t
    poly = jnp.full_like(t, SIN[-1])
    for coefficient in SIN[-2::-1]:
        poly = poly * t2 + coefficient
    return t + t * (t2 * poly)


def split(a):
    high = a.astype(BF16)
    return high, (a - high.astype(F32)).astype(BF16)


def dot(a, b):
    return jnp.dot(a, b, preferred_element_type=F32)


def dot3(a, b_high, b_low):
    rows = a.shape[0]
    a_high, a_low = split(a)
    both = dot(jnp.concatenate((a_high, a_low), axis=0), b_high)
    return both[:rows] + both[rows:] + dot(a_high, b_low)


def iota(shape, dimension):
    return lax.broadcasted_iota(jnp.int32, shape, dimension)


HOPS = (0, 1, 2, 1)
FAR_FIRST = sorted(range(1, 16), key=lambda d: -(HOPS[d % 4] + HOPS[d // 4]))


def kernel(
    frames, aperture, upper, lower,
    spectrum, wave,
    f, ap, up, lo, w, a, r1, zs, r3, t3, r_pair, q, r5, e_high, e_low, back_high, back_low,
    load_sem, pair_sem, sem1, sem3, send5, recv5,
):
    s = lax.axis_index("scan")
    c = lax.axis_index("det")
    y, z, x = s // 32, (s // 4) % 8, s % 4
    me = y * 4 + x

    def plane_peer(d):
        return ((y + d // 4) % 4) * 32 + z * 4 + (x + d % 4) % 4

    def z_peer(d):
        return s + ((z + d) % 8 - z) * 4

    loads = [
        pltpu.make_async_copy(upper, up, load_sem.at[0]),
        pltpu.make_async_copy(lower, lo, load_sem.at[1]),
        pltpu.make_async_copy(aperture, ap, load_sem.at[2]),
        pltpu.make_async_copy(frames.at[:, c], f.at[pl.ds(c * 128, 128)], load_sem.at[3]),
    ]
    for load in loads:
        load.start()

    barrier = pltpu.get_barrier_semaphore()

    def greet(scan, det):
        pl.semaphore_signal(barrier, inc=1, device_id=(scan, det), device_id_type=MESH)

    for d in (4, 3, 5, 2, 6, 1, 7):
        greet(z_peer(d), c)
    for d in FAR_FIRST:
        greet(plane_peer(d), c)
    greet(s, 1 - c)
    home = y // 2 == c

    @pl.when(jnp.logical_not(home))
    def _():
        for d in FAR_FIRST:
            greet(plane_peer(d), 1 - c)

    pl.semaphore_wait(barrier, 31 - jnp.where(home, 1, 0))

    swap = pltpu.make_async_remote_copy(
        src_ref=frames.at[:, 1 - c], dst_ref=f.at[pl.ds(c * 128, 128)],
        send_sem=pair_sem.at[0], recv_sem=pair_sem.at[1], device_id=(s, 1 - c), device_id_type=MESH,
    )
    swap.start()

    for load in loads[:3]:
        load.wait()
    pixel = iota((256, 128), 0)

    def count(j, total):
        plus = jnp.where(up[pl.ds(j, 1), :] == pixel, 1, 0)
        return total + plus - jnp.where(lo[pl.ds(j, 1), :] == pixel, 1, 0)

    counts = lax.fori_loop(0, 64, count, jnp.zeros((256, 128), jnp.int32))
    scaled = counts.astype(F32) * (64**-0.5 / 512)
    w[:128] = scaled[:128].T
    w[128:] = scaled[128:].T

    def weights(core):
        tiles = [w[pl.ds(core * 128 + 32 * (i // 4) + i % 4, 8, stride=4), :] for i in range(16)]
        inside = jnp.where(core == 0, ap[:, :128], ap[:, 128:]).astype(F32)
        weight = (jnp.concatenate(tiles, axis=0) * inside).astype(BF16)
        return jnp.concatenate((weight, weight), axis=1)

    flat = f.reshape(2048, 128)

    def weighted(weight, core, i):
        rows = [flat[pl.ds(core * 1024 + 4 * j + i, 128, stride=8), :] for j in range(2)]
        high, low = split(jnp.concatenate(rows, axis=1))
        return dot(weight, jnp.concatenate((high, low), axis=0)).reshape(16, 8, 256)

    near, far = weights(c), weights(1 - c)
    loads[3].wait()
    for i in range(4):
        a[:, i] = weighted(near, c, i)
    swap.wait_recv()

    def first_copy(d, h):
        target = ((y + d // 4) % 4) * 4 + (x + d % 4) % 4
        return pltpu.make_async_remote_copy(
            src_ref=a.at[target, pl.ds(2 * h, 2)], dst_ref=r1.at[d, pl.ds(2 * h, 2)],
            send_sem=sem1.at[0, h, d], recv_sem=sem1.at[1, h, d],
            device_id=(plane_peer(d), c), device_id_type=MESH,
        )

    for h in range(2):
        for i in range(2 * h, 2 * h + 2):
            a[:, i] = a[:, i] + weighted(far, 1 - c, i)
        for d in FAR_FIRST:
            first_copy(d, h).start()

    row, column = iota((64, 512), 0), iota((64, 512), 1)
    slot = column // 32
    chip = ((y - slot // 4) & 3) * 32 + 4 * z + ((x - slot % 4) & 3)
    place = 4 * chip + (column // 8) % 4
    block = y * 32 + x + 4 * (row // 8)
    left = cos512((4 * block + row % 4) * place + 32 * (row % 8 - row % 4))
    left_high, left_low = split(jnp.where(row // 8 == column % 8, left, 0.0))

    frequency = iota((256, 512), 1)
    wide = frequency % 256 + 256 * c
    table_high, table_low = split(cos512(wide * iota((256, 512), 0) - 128 * (frequency // 256)))
    e_high[...] = table_high
    e_low[...] = table_low

    n, source = iota((1024, 256), 1), iota((1024, 256), 0)
    source_block = (source // 256) * 32 + (source // 64) % 4 + 4 * ((source // 8) % 8)
    table_high, table_low = split(cos512(4 * source_block * (n % 128) - 128 * (n // 128)))
    back_high[...] = table_high
    back_low[...] = table_low

    part = jnp.zeros((64, 256), F32)
    for g in range(2):
        rows = []
        for d in range(8 * g, 8 * g + 8):
            if d:
                for h in range(2):
                    first_copy(d, h).wait_recv()
                rows.append(r1[d].reshape(32, 256))
            else:
                rows.append(a[me].reshape(32, 256))
        right_high, right_low = split(jnp.concatenate(rows, axis=0))
        columns = slice(256 * g, 256 * g + 256)
        both = dot(jnp.concatenate((left_high[:, columns], left_low[:, columns]), axis=0), right_high)
        part = part + (both[:64] + both[64:]) + dot(left_high[:, columns], right_low)

    turned = jnp.concatenate((part[:, :128], part[:, 128:]), axis=0).T
    for i in range(8):
        zs[i, :8] = part[8 * i : 8 * i + 8, :128]
        zs[i, 8:16] = part[8 * i : 8 * i + 8, 128:]
        zs[i, 16:] = turned[16 * i : 16 * i + 16]

    def third_copy(d):
        return pltpu.make_async_remote_copy(
            src_ref=zs.at[(z + d) % 8], dst_ref=r3.at[d], send_sem=sem3.at[0, d], recv_sem=sem3.at[1, d],
            device_id=(z_peer(d), c), device_id_type=MESH,
        )

    for d in (4, 3, 5, 2, 6, 1, 7):
        third_copy(d).start()
    total = zs[z]
    for d in (1, 7, 2, 6, 3, 5, 4):
        third_copy(d).wait_recv()
        total = total + r3[d]

    for i in range(4):
        q[i] = total[16 + 4 * i : 20 + 4 * i]

    def out_copy(i, core):
        chip = (2 * c + i // 4) * 32 + z * 4 + i % 4
        copy = pltpu.make_async_remote_copy(
            src_ref=q.at[i % 4], dst_ref=r5.at[me], send_sem=send5.at[2 * i + core], recv_sem=recv5.at[me],
            device_id=(chip, core), device_id_type=MESH,
        )
        return copy, jnp.logical_and(chip == s, c == core)

    for i in range(8):
        for core in range(2):
            copy, mine = out_copy(i, core)

            @pl.when(jnp.logical_not(mine))
            def _():
                copy.start()

            @pl.when(mine)
            def _():
                pltpu.make_async_copy(q.at[i % 4], r5.at[me], recv5.at[me]).start()

    band = jnp.concatenate((total[:8], total[8:16]), axis=1)
    t3[...] = band
    other = pltpu.make_async_remote_copy(
        src_ref=t3, dst_ref=r_pair, send_sem=pair_sem.at[2], recv_sem=pair_sem.at[3],
        device_id=(s, 1 - c), device_id_type=MESH,
    )
    other.start()
    lane, rho = iota((8, 256), 1), iota((8, 256), 0)
    angle = (rho % 4) * (lane + 256 * c) + 128 * (rho // 4)
    turn_real, turn_imag = cos512(angle), cos512(angle - 128)
    other.wait_recv()
    sums = dot3(jnp.concatenate((band, r_pair[...]), axis=0), e_high[...], e_low[...])
    sign = (1 - 2 * (lane % 2)).astype(F32)
    near, far = jnp.where(c == 0, 1.0, sign), jnp.where(c == 0, sign, 1.0)
    cosine = near * sums[:8, :256] + far * sums[8:, :256]
    sine = near * sums[:8, 256:] + far * sums[8:, 256:]
    side = jnp.where(rho < 4, -1.0, 1.0)
    result = cosine - side * jnp.concatenate((sine[4:], sine[:4]), axis=0)
    spectrum[0] = result[:4]
    spectrum[1] = result[4:]

    for i in range(16):
        pltpu.make_async_copy(q.at[0], r5.at[i], recv5.at[i]).wait()
    low_half = iota((4, 128), 1) < 64
    upper_y = y % 2 == 1
    mask = iota((8, 128), 0) == iota((8, 128), 1) % 8
    columns = []
    for j in range(8):
        even, odd = r5[2 * j], r5[2 * j + 1]
        even = jnp.where(upper_y, pltpu.roll(even, 64, 1), even)
        odd = jnp.where(upper_y, odd, pltpu.roll(odd, 64, 1))
        pair = jnp.where(low_half, even, odd)
        columns.append(jnp.concatenate([jnp.where(mask, pair[i : i + 1], 0.0) for i in range(4)], axis=0))
    moved = dot3(jnp.concatenate(columns, axis=1), back_high[...], back_low[...])
    reals, imags = [], []
    for i in range(4):
        tile = moved[8 * i : 8 * i + 8]
        sine = tile[:, 128:]
        pair = tile[:, :128] + side[:, :128] * jnp.concatenate((sine[4:], sine[:4]), axis=0)
        twice = jnp.concatenate((pair, pair), axis=1)
        reals.append(jnp.sum(twice * turn_real, axis=0, keepdims=True))
        imags.append(jnp.sum(twice * turn_imag, axis=0, keepdims=True))
    wave[0] = jnp.concatenate(reals, axis=0)
    wave[1] = jnp.concatenate(imags, axis=0)

    swap.wait_send()
    other.wait_send()
    for d in range(1, 16):
        first_copy(d, 0).wait_send()
        first_copy(d, 1).wait_send()
    for d in range(1, 8):
        third_copy(d).wait_send()
    for i in range(8):
        for core in range(2):
            copy, mine = out_copy(i, core)

            @pl.when(jnp.logical_not(mine))
            def _():
                copy.wait_send()


def per_device(frames, aperture, upper_pixels, lower_pixels):
    tiled = frames.reshape(128, 4, 4, 128).transpose(0, 2, 1, 3).reshape(128, 2, 8, 128)
    hbm = pl.BlockSpec(memory_space=pltpu.HBM)
    vmem = pl.BlockSpec(memory_space=pltpu.VMEM)
    dma = pltpu.SemaphoreType.DMA
    spectrum, wave = pl.pallas_call(
        kernel,
        out_shape=(jax.ShapeDtypeStruct((2, 4, 256), F32), jax.ShapeDtypeStruct((2, 4, 256), F32)),
        in_specs=[hbm] * 4,
        out_specs=(vmem, vmem),
        scratch_shapes=[
            pltpu.VMEM((256, 8, 128), F32),
            pltpu.VMEM((1, 256), jnp.int32),
            pltpu.VMEM((64, 128), jnp.int32),
            pltpu.VMEM((64, 128), jnp.int32),
            pltpu.VMEM((256, 128), F32),
            pltpu.VMEM((16, 4, 8, 256), F32),
            pltpu.VMEM((16, 4, 8, 256), F32),
            pltpu.VMEM((8, 32, 128), F32),
            pltpu.VMEM((8, 32, 128), F32),
            pltpu.VMEM((8, 256), F32),
            pltpu.VMEM((8, 256), F32),
            pltpu.VMEM((4, 4, 128), F32),
            pltpu.VMEM((16, 4, 128), F32),
            pltpu.VMEM((256, 512), BF16),
            pltpu.VMEM((256, 512), BF16),
            pltpu.VMEM((1024, 256), BF16),
            pltpu.VMEM((1024, 256), BF16),
            dma((4,)), dma((4,)), dma((2, 2, 16)), dma((2, 8)), dma((16,)), dma((16,)),
        ],
        compiler_params=pltpu.CompilerParams(
            collective_id=0, has_side_effects=True, vmem_limit_bytes=56 * 1024 * 1024
        ),
    )(tiled, aperture.reshape(1, 256), upper_pixels.T, lower_pixels.T)
    return spectrum, wave.transpose(0, 2, 1)


def solution(mesh):
    placed = (P("det", "scan", None), P(), P(), P())
    return jax.shard_map(
        per_device,
        mesh=mesh,
        in_specs=placed,
        out_specs=(P(None, "scan", "det"), P(None, "det", "scan")),
        check_vma=False,
    )
```

```python
import math

import jax
import jax.numpy as jnp
from jax import lax
from jax.experimental import pallas as pl
from jax.experimental.pallas import tpu as pltpu
from jax.sharding import PartitionSpec as P

MESH = pl.DeviceIdType.MESH
F32 = jnp.float32
BF16 = jnp.bfloat16
UNIT = 2.0 * math.pi / 512
SIN = (-1.0 / 6, 1.0 / 120, -1.0 / 5040, 1.0 / 362880, -1.0 / 39916800)


def cos512(m):
    m = m & 511
    t = (128 - jnp.minimum(m, 512 - m)).astype(F32) * UNIT
    t2 = t * t
    poly = jnp.full_like(t, SIN[-1])
    for coefficient in SIN[-2::-1]:
        poly = poly * t2 + coefficient
    return t + t * (t2 * poly)


def split(a):
    high = a.astype(BF16)
    return high, (a - high.astype(F32)).astype(BF16)


def dot(a, b):
    return jnp.dot(a, b, preferred_element_type=F32)


def dot3(a, b_high, b_low):
    rows = a.shape[0]
    a_high, a_low = split(a)
    both = dot(jnp.concatenate((a_high, a_low), axis=0), b_high)
    return both[:rows] + both[rows:] + dot(a_high, b_low)


def iota(shape, dimension):
    return lax.broadcasted_iota(jnp.int32, shape, dimension)


HOPS = (0, 1, 2, 1)
FAR_FIRST = sorted(range(1, 16), key=lambda d: -(HOPS[d % 4] + HOPS[d // 4]))


def kernel(
    frames, aperture, upper, lower,
    out,
    f, ap, up, lo, w, a, b, r1, zs, r3, t3, r_pair, q, r5, e_high, e_low, back_high, back_low,
    load_sem, swap_sem, pair_sem, sem1, sem3, send5, recv5,
):
    s = lax.axis_index("scan")
    c = lax.axis_index("det")
    y, z, x = s // 32, (s // 4) % 8, s % 4
    me = y * 4 + x

    def plane_peer(d):
        return ((y + d // 4) % 4) * 32 + z * 4 + (x + d % 4) % 4

    def z_peer(d):
        return s + ((z + d) % 8 - z) * 4

    loads = [
        pltpu.make_async_copy(upper, up, load_sem.at[0]),
        pltpu.make_async_copy(lower, lo, load_sem.at[1]),
        pltpu.make_async_copy(aperture, ap, load_sem.at[2]),
        pltpu.make_async_copy(frames, f, load_sem.at[3]),
    ]
    for load in loads:
        load.start()

    barrier = pltpu.get_barrier_semaphore()

    def greet(scan, det):
        pl.semaphore_signal(barrier, inc=1, device_id=(scan, det), device_id_type=MESH)

    home = y // 2 == c
    for hops in range(4, 0, -1):
        for d in range(1, 8):
            if min(d, 8 - d) == hops:
                greet(z_peer(d), c)
        peers = [d for d in FAR_FIRST if HOPS[d % 4] + HOPS[d // 4] == hops]
        for d in peers:
            greet(plane_peer(d), c)

        @pl.when(jnp.logical_not(home))
        def _():
            for d in peers:
                greet(plane_peer(d), 1 - c)

    greet(s, 1 - c)

    for load in loads[:3]:
        load.wait()
    pixel = (iota((128, 128), 0) + 128 * c).astype(F32).astype(BF16)
    one, none = jnp.ones((128, 128), BF16), jnp.zeros((128, 128), BF16)

    def row_of(ref, j):
        return jnp.broadcast_to(ref[pl.ds(j, 1), :], (128, 128)).astype(F32).astype(BF16)

    def count(j, total):
        total = total + jnp.where(row_of(up, j) == pixel, one, none)
        return total - jnp.where(row_of(lo, j) == pixel, one, none)

    counts = lax.fori_loop(0, 64, count, none, unroll=4)
    w[...] = (counts.astype(F32) * (64**-0.5 / 512)).T
    tiles = [w[pl.ds(32 * (i // 4) + i % 4, 8, stride=4), :] for i in range(16)]
    inside = jnp.where(c == 0, ap[:, :128], ap[:, 128:]).astype(F32)
    weight = (jnp.concatenate(tiles, axis=0) * inside).astype(BF16)
    weight = jnp.concatenate((weight, weight), axis=1)

    flat = f.reshape(2048, 128)

    def weighted(half):
        for i in range(4):
            rows = [flat[pl.ds(8 * half + 4 * j + i, 128, stride=16), :] for j in range(2)]
            high, low = split(jnp.concatenate(rows, axis=1))
            sums = dot(weight, jnp.concatenate((high, low), axis=0))
            a[half, :, i] = sums.reshape(16, 8, 256)

    loads[3].wait()
    weighted(1 - c)

    pl.semaphore_wait(barrier, 31 - jnp.where(home, 1, 0))

    def plane_index(d):
        return ((y + d // 4) % 4) * 4 + (x + d % 4) % 4

    def swap_copy(d):
        return pltpu.make_async_remote_copy(
            src_ref=a.at[1 - c, plane_index(d)], dst_ref=b.at[d], send_sem=swap_sem.at[0, d], recv_sem=swap_sem.at[1, d],
            device_id=(s, 1 - c), device_id_type=MESH,
        )

    for d in FAR_FIRST + [0]:
        swap_copy(d).start()
    weighted(c)

    def first_copy(d):
        return pltpu.make_async_remote_copy(
            src_ref=b.at[d], dst_ref=r1.at[d], send_sem=sem1.at[0, d], recv_sem=sem1.at[1, d],
            device_id=(plane_peer(d), c), device_id_type=MESH,
        )

    for d in FAR_FIRST + [0]:
        swap_copy(d).wait_recv()
        b[d] = b[d] + a[c, plane_index(d)]
        if d:
            first_copy(d).start()

    row, column = iota((64, 512), 0), iota((64, 512), 1)
    slot = column // 32
    chip = ((y - slot // 4) & 3) * 32 + 4 * z + ((x - slot % 4) & 3)
    place = 4 * chip + (column // 8) % 4
    block = y * 32 + x + 4 * (row // 8)
    left = cos512((4 * block + row % 4) * place + 32 * (row % 8 - row % 4))
    left_high, left_low = split(jnp.where(row // 8 == column % 8, left, 0.0))

    frequency = iota((256, 512), 1)
    wide = frequency % 256 + 256 * c
    table_high, table_low = split(cos512(wide * iota((256, 512), 0) - 128 * (frequency // 256)))
    e_high[...] = table_high
    e_low[...] = table_low

    n, source = iota((1024, 256), 1), iota((1024, 256), 0)
    source_block = (source // 256) * 32 + (source // 64) % 4 + 4 * ((source // 8) % 8)
    table_high, table_low = split(cos512(4 * source_block * (n % 128) - 128 * (n // 128)))
    back_high[...] = table_high
    back_low[...] = table_low

    part = jnp.zeros((64, 256), F32)
    for g in range(2):
        rows = []
        for d in range(8 * g, 8 * g + 8):
            if d:
                first_copy(d).wait_recv()
                rows.append(r1[d].reshape(32, 256))
            else:
                rows.append(b[0].reshape(32, 256))
        right_high, right_low = split(jnp.concatenate(rows, axis=0))
        columns = slice(256 * g, 256 * g + 256)
        both = dot(jnp.concatenate((left_high[:, columns], left_low[:, columns]), axis=0), right_high)
        part = part + (both[:64] + both[64:]) + dot(left_high[:, columns], right_low)

    turned = jnp.concatenate((part[:, :128], part[:, 128:]), axis=0).T
    for i in range(8):
        zs[i, :8] = part[8 * i : 8 * i + 8, :128]
        zs[i, 8:16] = part[8 * i : 8 * i + 8, 128:]
        zs[i, 16:] = turned[16 * i : 16 * i + 16]

    def third_copy(d, h):
        rows = pl.ds(16 * h, 16)
        return pltpu.make_async_remote_copy(
            src_ref=zs.at[(z + d) % 8, rows], dst_ref=r3.at[d, rows],
            send_sem=sem3.at[0, h, d], recv_sem=sem3.at[1, h, d],
            device_id=(z_peer(d), c), device_id_type=MESH,
        )

    def z_sum(h):
        rows = pl.ds(16 * h, 16)
        total = zs[z, rows]
        for d in (1, 7, 2, 6, 3, 5, 4):
            third_copy(d, h).wait_recv()
            total = total + r3[d, rows]
        return total

    for h in (1, 0):
        for d in (4, 3, 5, 2, 6, 1, 7):
            third_copy(d, h).start()

    total = z_sum(1)
    for i in range(4):
        q[i] = total[4 * i : 4 * i + 4]

    def out_copy(i, core):
        chip = (2 * c + i // 4) * 32 + z * 4 + i % 4
        copy = pltpu.make_async_remote_copy(
            src_ref=q.at[i % 4], dst_ref=r5.at[me], send_sem=send5.at[2 * i + core], recv_sem=recv5.at[me],
            device_id=(chip, core), device_id_type=MESH,
        )
        return copy, jnp.logical_and(chip == s, c == core)

    for i in range(8):
        for core in range(2):
            copy, mine = out_copy(i, core)

            @pl.when(jnp.logical_not(mine))
            def _():
                copy.start()

            @pl.when(mine)
            def _():
                pltpu.make_async_copy(q.at[i % 4], r5.at[me], recv5.at[me]).start()

    total = z_sum(0)
    band = jnp.concatenate((total[:8], total[8:]), axis=1)
    t3[...] = band
    other = pltpu.make_async_remote_copy(
        src_ref=t3, dst_ref=r_pair, send_sem=pair_sem.at[0], recv_sem=pair_sem.at[1],
        device_id=(s, 1 - c), device_id_type=MESH,
    )
    other.start()
    lane, rho = iota((8, 256), 1), iota((8, 256), 0)
    angle = (rho % 4) * (lane + 256 * c) + 128 * (rho // 4)
    turn_real, turn_imag = cos512(angle), cos512(angle - 128)
    other.wait_recv()
    sums = dot3(jnp.concatenate((band, r_pair[...]), axis=0), e_high[...], e_low[...])
    sign = (1 - 2 * (lane % 2)).astype(F32)
    near, far = jnp.where(c == 0, 1.0, sign), jnp.where(c == 0, sign, 1.0)
    cosine = near * sums[:8, :256] + far * sums[8:, :256]
    sine = near * sums[:8, 256:] + far * sums[8:, 256:]
    side = jnp.where(rho < 4, -1.0, 1.0)
    result = cosine - side * jnp.concatenate((sine[4:], sine[:4]), axis=0)
    out[0] = result[:4]
    out[1] = result[4:]

    for i in range(16):
        pltpu.make_async_copy(q.at[0], r5.at[i], recv5.at[i]).wait()
    low_half = iota((4, 128), 1) < 64
    upper_y = y % 2 == 1
    mask = iota((8, 128), 0) == iota((8, 128), 1) % 8
    columns = []
    for j in range(8):
        even, odd = r5[2 * j], r5[2 * j + 1]
        even = jnp.where(upper_y, pltpu.roll(even, 64, 1), even)
        odd = jnp.where(upper_y, odd, pltpu.roll(odd, 64, 1))
        pair = jnp.where(low_half, even, odd)
        columns.append(jnp.concatenate([jnp.where(mask, pair[i : i + 1], 0.0) for i in range(4)], axis=0))
    moved = dot3(jnp.concatenate(columns, axis=1), back_high[...], back_low[...])
    reals, imags = [], []
    for i in range(4):
        tile = moved[8 * i : 8 * i + 8]
        sine = tile[:, 128:]
        pair = tile[:, :128] + side[:, :128] * jnp.concatenate((sine[4:], sine[:4]), axis=0)
        twice = jnp.concatenate((pair, pair), axis=1)
        reals.append(jnp.sum(twice * turn_real, axis=0, keepdims=True))
        imags.append(jnp.sum(twice * turn_imag, axis=0, keepdims=True))
    out[2] = jnp.concatenate(reals, axis=0)
    out[3] = jnp.concatenate(imags, axis=0)

    for d in range(16):
        swap_copy(d).wait_send()
    other.wait_send()
    for d in range(1, 16):
        first_copy(d).wait_send()
    for d in range(1, 8):
        third_copy(d, 0).wait_send()
        third_copy(d, 1).wait_send()
    for i in range(8):
        for core in range(2):
            copy, mine = out_copy(i, core)

            @pl.when(jnp.logical_not(mine))
            def _():
                copy.wait_send()


def per_device(frames, aperture, upper_pixels, lower_pixels):
    tiled = frames.reshape(128, 4, 4, 128).transpose(0, 2, 1, 3).reshape(128, 2, 8, 128)
    operands = (tiled, aperture.reshape(1, 256), upper_pixels.T, lower_pixels.T)
    hbm = pl.BlockSpec(memory_space=pltpu.HBM)
    dma = pltpu.SemaphoreType.DMA
    both = pl.pallas_call(
        kernel,
        out_shape=pltpu.VMEM((4, 4, 256), F32),
        in_specs=[hbm] * 4,
        out_specs=pl.BlockSpec(memory_space=pltpu.VMEM),
        scratch_shapes=[
            pltpu.VMEM((128, 2, 8, 128), F32),
            pltpu.VMEM((1, 256), jnp.int32),
            pltpu.VMEM((64, 128), jnp.int32),
            pltpu.VMEM((64, 128), jnp.int32),
            pltpu.VMEM((128, 128), F32),
            pltpu.VMEM((2, 16, 4, 8, 256), F32),
            pltpu.VMEM((16, 4, 8, 256), F32),
            pltpu.VMEM((16, 4, 8, 256), F32),
            pltpu.VMEM((8, 32, 128), F32),
            pltpu.VMEM((8, 32, 128), F32),
            pltpu.VMEM((8, 256), F32),
            pltpu.VMEM((8, 256), F32),
            pltpu.VMEM((4, 4, 128), F32),
            pltpu.VMEM((16, 4, 128), F32),
            pltpu.VMEM((256, 512), BF16),
            pltpu.VMEM((256, 512), BF16),
            pltpu.VMEM((1024, 256), BF16),
            pltpu.VMEM((1024, 256), BF16),
            dma((4,)), dma((2, 16)), dma((2,)), dma((2, 16)), dma((2, 2, 8)), dma((16,)), dma((16,)),
        ],
        compiler_params=pltpu.CompilerParams(
            collective_id=0, has_side_effects=True, vmem_limit_bytes=32 * 1024 * 1024
        ),
    )(*[pltpu.with_memory_space_constraint(operand, pltpu.HBM) for operand in operands])
    return both[:2], both[2:].transpose(0, 2, 1)


def solution(mesh):
    placed = (P("det", "scan", None), P(), P(), P())
    return jax.shard_map(
        per_device,
        mesh=mesh,
        in_specs=placed,
        out_specs=(P(None, "scan", "det"), P(None, "det", "scan")),
        check_vma=False,
    )
```

```python
import math

import jax
import jax.numpy as jnp
from jax import lax
from jax.experimental import pallas as pl
from jax.experimental.pallas import tpu as pltpu
from jax.sharding import PartitionSpec as P

MESH = pl.DeviceIdType.MESH
F32 = jnp.float32
BF16 = jnp.bfloat16
UNIT = 2.0 * math.pi / 512
SIN = (-1.0 / 6, 1.0 / 120, -1.0 / 5040, 1.0 / 362880, -1.0 / 39916800)


def cos512(m):
    m = m & 511
    t = (128 - jnp.minimum(m, 512 - m)).astype(F32) * UNIT
    t2 = t * t
    poly = jnp.full_like(t, SIN[-1])
    for coefficient in SIN[-2::-1]:
        poly = poly * t2 + coefficient
    return t + t * (t2 * poly)


def split(a):
    high = a.astype(BF16)
    return high, (a - high.astype(F32)).astype(BF16)


def dot(a, b):
    return jnp.dot(a, b, preferred_element_type=F32)


def dot3(a, b_high, b_low):
    rows = a.shape[0]
    a_high, a_low = split(a)
    both = dot(jnp.concatenate((a_high, a_low), axis=0), b_high)
    return both[:rows] + both[rows:] + dot(a_high, b_low)


def iota(shape, dimension):
    return lax.broadcasted_iota(jnp.int32, shape, dimension)


LOADS = 4


def kernel(
    frames, aperture, upper, lower,
    out,
    f, ap, up, lo, w, a, b, r1, zs, r3, q, r5, t, r6, e_high, e_low, back_high, back_low,
    load_sem, swap_sem, sem1, sem3, send5, recv5, send6, recv6,
):
    s = lax.axis_index("scan")
    c = lax.axis_index("det")
    y, z, x = s // 32, (s // 4) % 8, s % 4
    me = y * 4 + x
    home = y // 2 == c

    def chip_at(cy, cx):
        return cy * 32 + z * 4 + cx

    first_row = jnp.where(home, 1 - y % 2, y % 2)
    TARGETS = [(dx, j, core) for dx in (2, 1, 3, 0) for j in range(2) for core in range(2)]

    def target(dx, j):
        return (x + dx) % 4, first_row * (1 - j) + (1 - first_row) * j

    def z_peer(d):
        return s + ((z + d) % 8 - z) * 4

    loads = [
        pltpu.make_async_copy(upper, up, load_sem.at[0]),
        pltpu.make_async_copy(lower, lo, load_sem.at[1]),
        pltpu.make_async_copy(aperture, ap, load_sem.at[2]),
    ]
    for i in range(LOADS):
        pixels = pl.ds(i * (128 // LOADS), 128 // LOADS)
        loads.append(pltpu.make_async_copy(frames.at[pixels], f.at[pixels], load_sem.at[3 + i]))
    for load in loads:
        load.start()

    barrier = pltpu.get_barrier_semaphore()

    def greet(scan, det):
        pl.semaphore_signal(barrier, inc=1, device_id=(scan, det), device_id_type=MESH)

    for d in (4, 3, 5, 2, 6, 1, 7):
        greet(z_peer(d), c)
    for dx in (2, 1, 3, 0):
        for dy in (2, 1, 3, 0):

            @pl.when(jnp.logical_or(jnp.logical_not(home), dx + dy > 0))
            def _():
                greet(chip_at((y + dy) % 4, (x + dx) % 4), y // 2)

        @pl.when(jnp.logical_or(home, dx > 0))
        def _():
            greet(chip_at(y, (x + dx) % 4), 1 - y // 2)

    for load in loads[:3]:
        load.wait()
    pixel = (iota((128, 128), 0) + 128 * c).astype(F32).astype(BF16)
    one, none = jnp.ones((128, 128), BF16), jnp.zeros((128, 128), BF16)

    def row_of(ref, j):
        return jnp.broadcast_to(ref[pl.ds(j, 1), :], (128, 128)).astype(F32).astype(BF16)

    def count(j, total):
        total = total + jnp.where(row_of(up, j) == pixel, one, none)
        return total - jnp.where(row_of(lo, j) == pixel, one, none)

    counts = lax.fori_loop(0, 64, count, none, unroll=4)
    w[...] = (counts.astype(F32) * (64**-0.5 / 512)).T
    tiles = [w[pl.ds(32 * (i % 4) + i // 4, 8, stride=4), :] for i in range(16)]
    inside = jnp.where(c == 0, ap[:, :128], ap[:, 128:]).astype(F32)
    weight = (jnp.concatenate(tiles, axis=0) * inside).astype(BF16)
    weight = jnp.concatenate((weight, weight), axis=1)

    flat = f.reshape(2048, 128)

    def weighted(half):
        for i in range(4):
            rows = [flat[pl.ds(8 * half + 4 * j + i, 128, stride=16), :] for j in range(2)]
            high, low = split(jnp.concatenate(rows, axis=1))
            sums = dot(weight, jnp.concatenate((high, low), axis=0))
            for j in range(2):
                a[half, j, :, :, i] = sums[:, 128 * j : 128 * j + 128].reshape(4, 2, 16, 128)

    for load in loads[3:]:
        load.wait()
    weighted(1 - c)

    pl.semaphore_wait(barrier, jnp.where(home, 22, 30))

    def swap_copy(i):
        dx, j, core = TARGETS[i]
        cx, row = target(dx, j)
        far_row = jnp.where(home, y % 2, 1 - y % 2) * (1 - j) + jnp.where(home, 1 - y % 2, y % 2) * j
        return pltpu.make_async_remote_copy(
            src_ref=a.at[1 - c, far_row, cx, core], dst_ref=b.at[i],
            send_sem=swap_sem.at[0, i], recv_sem=swap_sem.at[1, i], device_id=(s, 1 - c), device_id_type=MESH,
        )

    for i in range(16):
        swap_copy(i).start()
    weighted(c)

    def first_copy(i):
        dx, j, core = TARGETS[i]
        cx, row = target(dx, j)
        chip = chip_at(2 * c + row, cx)
        copy = pltpu.make_async_remote_copy(
            src_ref=b.at[i], dst_ref=r1.at[me], send_sem=sem1.at[0, i], recv_sem=sem1.at[1, me],
            device_id=(chip, core), device_id_type=MESH,
        )
        return copy, jnp.logical_and(chip == s, c == core)

    for i, (dx, j, core) in enumerate(TARGETS):
        cx, row = target(dx, j)
        swap_copy(i).wait_recv()
        b[i] = b[i] + a[c, row, cx, core]
        copy, mine = first_copy(i)

        @pl.when(jnp.logical_not(mine))
        def _():
            copy.start()

        @pl.when(mine)
        def _():
            pltpu.make_async_copy(b.at[i], r1.at[me], sem1.at[1, me]).start()

    row, column = iota((64, 512), 0), iota((64, 512), 1)
    chip = (column // 128) * 32 + 4 * z + (column // 32) % 4
    place = 4 * chip + (column // 8) % 4
    same = row // 8 == column % 8
    lefts = []
    for i in range(2):
        block = (2 * c + i) * 32 + x + 4 * (row // 8)
        left = cos512((4 * block + row % 4) * place + 32 * (row % 8 - row % 4))
        lefts.append(split(jnp.where(same, left, 0.0)))

    frequency = iota((256, 512), 1)
    wide = frequency % 256 + 256 * c
    table_high, table_low = split(cos512(wide * iota((256, 512), 0) - 128 * (frequency // 256)))
    e_high[...] = table_high
    e_low[...] = table_low

    n, source = iota((1024, 256), 1), iota((1024, 256), 0)
    source_block = ((source // 64) % 4) * 32 + source // 256 + 4 * ((source // 8) % 8)
    table_high, table_low = split(cos512(4 * source_block * (n % 128) - 128 * (n // 128)))
    back_high[...] = table_high
    back_low[...] = table_low

    for i in range(16):
        pltpu.make_async_copy(b.at[0], r1.at[i], sem1.at[1, i]).wait()
    parts = []
    for i in range(2):
        right = jnp.concatenate([r1[k, :, 8 * i : 8 * i + 8].reshape(32, 128) for k in range(16)], axis=0)
        right_high, right_low = split(right)
        left_high, left_low = lefts[i]
        both = dot(jnp.concatenate((left_high, left_low), axis=0), right_high)
        parts.append((both[:64] + both[64:]) + dot(left_high, right_low))

    turned = jnp.concatenate(parts, axis=0).T
    for i in range(8):
        zs[i, :8] = parts[0][8 * i : 8 * i + 8]
        zs[i, 8:16] = parts[1][8 * i : 8 * i + 8]
        zs[i, 16:] = turned[16 * i : 16 * i + 16]

    def third_copy(d, h):
        rows = pl.ds(16 * h, 16)
        return pltpu.make_async_remote_copy(
            src_ref=zs.at[(z + d) % 8, rows], dst_ref=r3.at[d, rows],
            send_sem=sem3.at[0, h, d], recv_sem=sem3.at[1, h, d],
            device_id=(z_peer(d), c), device_id_type=MESH,
        )

    def z_sum(h):
        rows = pl.ds(16 * h, 16)
        total = zs[z, rows]
        for d in (1, 7, 2, 6, 3, 5, 4):
            third_copy(d, h).wait_recv()
            total = total + r3[d, rows]
        return total

    for h in (1, 0):
        for d in (4, 3, 5, 2, 6, 1, 7):
            third_copy(d, h).start()

    total = z_sum(1)
    for i in range(4):
        q[i] = total[4 * i : 4 * i + 4]

    def out_copy(dx, core):
        cx = (x + dx) % 4
        copy = pltpu.make_async_remote_copy(
            src_ref=q.at[cx], dst_ref=r5.at[2 * x + c], send_sem=send5.at[dx, core], recv_sem=recv5.at[2 * x + c],
            device_id=(chip_at(y, cx), core), device_id_type=MESH,
        )
        return copy, jnp.logical_and(dx == 0, c == core)

    for dx in (2, 1, 3, 0):
        for core in range(2):
            copy, mine = out_copy(dx, core)

            @pl.when(jnp.logical_not(mine))
            def _():
                copy.start()

            @pl.when(mine)
            def _():
                pltpu.make_async_copy(q.at[x], r5.at[2 * x + c], recv5.at[2 * x + c]).start()

    total = z_sum(0)
    for i in range(2):
        t[i] = total[8 * i : 8 * i + 8]

    def band_copy(j, core):
        row = target(0, j)[1]
        chip = chip_at(2 * c + row, x)
        copy = pltpu.make_async_remote_copy(
            src_ref=t.at[row], dst_ref=r6.at[y], send_sem=send6.at[j, core], recv_sem=recv6.at[y],
            device_id=(chip, core), device_id_type=MESH,
        )
        return copy, jnp.logical_and(chip == s, c == core)

    for j in range(2):
        for core in range(2):
            copy, mine = band_copy(j, core)

            @pl.when(jnp.logical_not(mine))
            def _():
                copy.start()

            @pl.when(mine)
            def _():
                pltpu.make_async_copy(t.at[y % 2], r6.at[y], recv6.at[y]).start()

    lane, rho = iota((8, 256), 1), iota((8, 256), 0)
    angle = (rho % 4) * (lane + 256 * c) + 128 * (rho // 4)
    turn_real, turn_imag = cos512(angle), cos512(angle - 128)
    side = jnp.where(rho < 4, -1.0, 1.0)

    for i in range(8):
        pltpu.make_async_copy(q.at[0], r5.at[i], recv5.at[i]).wait()
    mask = iota((8, 128), 0) == iota((8, 128), 1) % 8
    columns = []
    for j in range(8):
        rows = r5[j]
        columns.append(jnp.concatenate([jnp.where(mask, rows[i : i + 1], 0.0) for i in range(4)], axis=0))
    moved = dot3(jnp.concatenate(columns, axis=1), back_high[...], back_low[...])
    reals, imags = [], []
    for i in range(4):
        tile = moved[8 * i : 8 * i + 8]
        sine = tile[:, 128:]
        pair = tile[:, :128] + side[:, :128] * jnp.concatenate((sine[4:], sine[:4]), axis=0)
        twice = jnp.concatenate((pair, pair), axis=1)
        reals.append(jnp.sum(twice * turn_real, axis=0, keepdims=True))
        imags.append(jnp.sum(twice * turn_imag, axis=0, keepdims=True))
    out[2] = jnp.concatenate(reals, axis=0)
    out[3] = jnp.concatenate(imags, axis=0)

    for i in range(4):
        pltpu.make_async_copy(t.at[0], r6.at[i], recv6.at[i]).wait()
    halves = [jnp.concatenate((r6[2 * i], r6[2 * i + 1]), axis=1) for i in range(2)]
    sums = dot3(jnp.concatenate(halves, axis=0), e_high[...], e_low[...])
    sign = (1 - 2 * (lane % 2)).astype(F32)
    cosine = sums[:8, :256] + sign * sums[8:, :256]
    sine = sums[:8, 256:] + sign * sums[8:, 256:]
    result = cosine - side * jnp.concatenate((sine[4:], sine[:4]), axis=0)
    out[0] = result[:4]
    out[1] = result[4:]

    for i in range(16):
        swap_copy(i).wait_send()
    for d in range(1, 8):
        third_copy(d, 0).wait_send()
        third_copy(d, 1).wait_send()
    copies = [first_copy(i) for i in range(16)]
    copies += [out_copy(dx, core) for dx in range(4) for core in range(2)]
    copies += [band_copy(j, core) for j in range(2) for core in range(2)]
    for copy, mine in copies:

        @pl.when(jnp.logical_not(mine))
        def _():
            copy.wait_send()


def per_device(frames, aperture, upper_pixels, lower_pixels):
    tiled = frames.reshape(128, 4, 4, 128).transpose(0, 2, 1, 3).reshape(128, 2, 8, 128)
    operands = (tiled, aperture.reshape(1, 256), upper_pixels.T, lower_pixels.T)
    hbm = pl.BlockSpec(memory_space=pltpu.HBM)
    dma = pltpu.SemaphoreType.DMA
    both = pl.pallas_call(
        kernel,
        out_shape=pltpu.VMEM((4, 4, 256), F32),
        in_specs=[hbm] * 4,
        out_specs=pl.BlockSpec(memory_space=pltpu.VMEM),
        scratch_shapes=[
            pltpu.VMEM((128, 2, 8, 128), F32),
            pltpu.VMEM((1, 256), jnp.int32),
            pltpu.VMEM((64, 128), jnp.int32),
            pltpu.VMEM((64, 128), jnp.int32),
            pltpu.VMEM((128, 128), F32),
            pltpu.VMEM((2, 2, 4, 2, 4, 16, 128), F32),
            pltpu.VMEM((16, 4, 16, 128), F32),
            pltpu.VMEM((16, 4, 16, 128), F32),
            pltpu.VMEM((8, 32, 128), F32),
            pltpu.VMEM((8, 32, 128), F32),
            pltpu.VMEM((4, 4, 128), F32),
            pltpu.VMEM((8, 4, 128), F32),
            pltpu.VMEM((2, 8, 128), F32),
            pltpu.VMEM((4, 8, 128), F32),
            pltpu.VMEM((256, 512), BF16),
            pltpu.VMEM((256, 512), BF16),
            pltpu.VMEM((1024, 256), BF16),
            pltpu.VMEM((1024, 256), BF16),
            dma((3 + LOADS,)), dma((2, 16)), dma((2, 16)), dma((2, 2, 8)), dma((4, 2)), dma((8,)), dma((2, 2)), dma((4,)),
        ],
        compiler_params=pltpu.CompilerParams(
            collective_id=0, has_side_effects=True, vmem_limit_bytes=32 * 1024 * 1024
        ),
    )(*[pltpu.with_memory_space_constraint(operand, pltpu.HBM) for operand in operands])
    return both[:2], both[2:].transpose(0, 2, 1)


def solution(mesh):
    placed = (P("det", "scan", None), P(), P(), P())
    return jax.shard_map(
        per_device,
        mesh=mesh,
        in_specs=placed,
        out_specs=(P(None, "scan", "det"), P(None, "det", "scan")),
        check_vma=False,
    )
```

```python
import math

import jax
import jax.numpy as jnp
from jax import lax
from jax.experimental import pallas as pl
from jax.experimental.pallas import tpu as pltpu
from jax.sharding import PartitionSpec as P

MESH = pl.DeviceIdType.MESH
F32 = jnp.float32
BF16 = jnp.bfloat16
UNIT = 2.0 * math.pi / 512
SIN = (-1.0 / 6, 1.0 / 120, -1.0 / 5040, 1.0 / 362880, -1.0 / 39916800)


def cos512(m):
    m = m & 511
    t = (128 - jnp.minimum(m, 512 - m)).astype(F32) * UNIT
    t2 = t * t
    poly = jnp.full_like(t, SIN[-1])
    for coefficient in SIN[-2::-1]:
        poly = poly * t2 + coefficient
    return t + t * (t2 * poly)


def split(a):
    high = a.astype(BF16)
    return high, (a - high.astype(F32)).astype(BF16)


def dot(a, b):
    return jnp.dot(a, b, preferred_element_type=F32)


def dot3(a, b_high, b_low):
    rows = a.shape[0]
    a_high, a_low = split(a)
    both = dot(jnp.concatenate((a_high, a_low), axis=0), b_high)
    return both[:rows] + both[rows:] + dot(a_high, b_low)


def iota(shape, dimension):
    return lax.broadcasted_iota(jnp.int32, shape, dimension)


LOADS = 4


def kernel(
    frames, aperture, upper, lower,
    out,
    f, ap, up, lo, w, a, b, r1, zs, r3, q, r5, t, r6, e_high, e_low, back_high, back_low,
    load_sem, swap_sem, sem1, sem3, sem5, sem6,
):
    s = lax.axis_index("scan")
    c = lax.axis_index("det")
    y, z, x = s // 32, (s // 4) % 8, s % 4
    me = y * 4 + x
    home = y // 2 == c

    def chip_at(cy, cx):
        return cy * 32 + z * 4 + cx

    first_row = jnp.where(home, 1 - y % 2, y % 2)
    TARGETS = [(dx, j, core) for dx in (2, 1, 3, 0) for j in range(2) for core in range(2)]

    def target(dx, j):
        return (x + dx) % 4, first_row * (1 - j) + (1 - first_row) * j

    def z_peer(d):
        return s + ((z + d) % 8 - z) * 4

    loads = [
        pltpu.make_async_copy(upper, up, load_sem.at[0]),
        pltpu.make_async_copy(lower, lo, load_sem.at[1]),
        pltpu.make_async_copy(aperture, ap, load_sem.at[2]),
    ]
    for i in range(LOADS):
        pixels = pl.ds(i * (128 // LOADS), 128 // LOADS)
        loads.append(pltpu.make_async_copy(frames.at[pixels], f.at[pixels], load_sem.at[3 + i]))
    for load in loads:
        load.start()

    barrier = pltpu.get_barrier_semaphore()

    def greet(scan, det):
        pl.semaphore_signal(barrier, inc=1, device_id=(scan, det), device_id_type=MESH)

    for d in (4, 3, 5, 2, 6, 1, 7):
        greet(z_peer(d), c)
    for dx in (2, 1, 3, 0):
        for dy in (2, 1, 3, 0):

            @pl.when(jnp.logical_or(jnp.logical_not(home), dx + dy > 0))
            def _():
                greet(chip_at((y + dy) % 4, (x + dx) % 4), y // 2)

        @pl.when(jnp.logical_or(home, dx > 0))
        def _():
            greet(chip_at(y, (x + dx) % 4), 1 - y // 2)

    for load in loads[:3]:
        load.wait()
    pixel = (iota((128, 128), 0) + 128 * c).astype(F32).astype(BF16)
    one, none = jnp.ones((128, 128), BF16), jnp.zeros((128, 128), BF16)

    def row_of(ref, j):
        return jnp.broadcast_to(ref[pl.ds(j, 1), :], (128, 128)).astype(F32).astype(BF16)

    def count(j, total):
        total = total + jnp.where(row_of(up, j) == pixel, one, none)
        return total - jnp.where(row_of(lo, j) == pixel, one, none)

    counts = lax.fori_loop(0, 64, count, none, unroll=4)
    w[...] = (counts.astype(F32) * (64**-0.5 / 512)).T
    tiles = [w[pl.ds(32 * (i % 4) + i // 4, 8, stride=4), :] for i in range(16)]
    inside = jnp.where(c == 0, ap[:, :128], ap[:, 128:]).astype(F32)
    weight = (jnp.concatenate(tiles, axis=0) * inside).astype(BF16)
    weight = jnp.concatenate((weight, weight), axis=1)

    flat = f.reshape(2048, 128)

    def weighted(half):
        for i in range(4):
            rows = [flat[pl.ds(8 * half + 4 * j + i, 128, stride=16), :] for j in range(2)]
            high, low = split(jnp.concatenate(rows, axis=1))
            sums = dot(weight, jnp.concatenate((high, low), axis=0))
            for j in range(2):
                a[half, j, :, :, i] = sums[:, 128 * j : 128 * j + 128].reshape(4, 2, 16, 128)

    for load in loads[3:]:
        load.wait()
    weighted(1 - c)
    weighted(c)

    pl.semaphore_wait(barrier, jnp.where(home, 22, 30))

    def swap_copy(i):
        dx, j, core = TARGETS[i]
        cx, row = target(dx, j)
        far_row = jnp.where(home, y % 2, 1 - y % 2) * (1 - j) + jnp.where(home, 1 - y % 2, y % 2) * j
        return pltpu.make_async_remote_copy(
            src_ref=a.at[1 - c, far_row, cx, core], dst_ref=b.at[i],
            send_sem=swap_sem.at[16], recv_sem=swap_sem.at[i], device_id=(s, 1 - c), device_id_type=MESH,
        )

    for i in range(16):
        swap_copy(i).start()

    def first_copy(i):
        dx, j, core = TARGETS[i]
        cx, row = target(dx, j)
        chip = chip_at(2 * c + row, cx)
        copy = pltpu.make_async_remote_copy(
            src_ref=b.at[i], dst_ref=r1.at[me], send_sem=sem1.at[0], recv_sem=sem1.at[1],
            device_id=(chip, core), device_id_type=MESH,
        )
        return copy, jnp.logical_and(chip == s, c == core)

    for i, (dx, j, core) in enumerate(TARGETS):
        cx, row = target(dx, j)
        swap_copy(i).wait_recv()
        b[i] = b[i] + a[c, row, cx, core]
        copy, mine = first_copy(i)
        if dx or not j:
            copy.start()
        else:

            @pl.when(jnp.logical_not(mine))
            def _():
                copy.start()

            @pl.when(mine)
            def _():
                pltpu.make_async_copy(b.at[i], r1.at[me], sem1.at[1]).start()

    row, column = iota((64, 512), 0), iota((64, 512), 1)
    chip = (column // 128) * 32 + 4 * z + (column // 32) % 4
    place = 4 * chip + (column // 8) % 4
    same = row // 8 == column % 8
    lefts = []
    for i in range(2):
        block = (2 * c + i) * 32 + x + 4 * (row // 8)
        left = cos512((4 * block + row % 4) * place + 32 * (row % 8 - row % 4))
        lefts.append(split(jnp.where(same, left, 0.0)))

    frequency = iota((256, 512), 1)
    wide = frequency % 256 + 256 * c
    table_high, table_low = split(cos512(wide * iota((256, 512), 0) - 128 * (frequency // 256)))
    e_high[...] = table_high
    e_low[...] = table_low

    n, source = iota((1024, 256), 1), iota((1024, 256), 0)
    source_block = ((source // 64) % 4) * 32 + source // 256 + 4 * ((source // 8) % 8)
    table_high, table_low = split(cos512(4 * source_block * (n % 128) - 128 * (n // 128)))
    back_high[...] = table_high
    back_low[...] = table_low

    pltpu.make_async_copy(r1, r1, sem1.at[1]).wait()
    parts = []
    for i in range(2):
        right = jnp.concatenate([r1[k, :, 8 * i : 8 * i + 8].reshape(32, 128) for k in range(16)], axis=0)
        right_high, right_low = split(right)
        left_high, left_low = lefts[i]
        both = dot(jnp.concatenate((left_high, left_low), axis=0), right_high)
        parts.append((both[:64] + both[64:]) + dot(left_high, right_low))

    turned = jnp.concatenate(parts, axis=0).T
    for i in range(8):
        zs[i, :8] = parts[0][8 * i : 8 * i + 8]
        zs[i, 8:16] = parts[1][8 * i : 8 * i + 8]
        zs[i, 16:] = turned[16 * i : 16 * i + 16]

    def third_copy(d, h):
        rows = pl.ds(16 * h, 16)
        return pltpu.make_async_remote_copy(
            src_ref=zs.at[(z + d) % 8, rows], dst_ref=r3.at[d, rows],
            send_sem=sem3.at[h, 0], recv_sem=sem3.at[h, d],
            device_id=(z_peer(d), c), device_id_type=MESH,
        )

    def z_sum(h):
        rows = pl.ds(16 * h, 16)
        total = zs[z, rows]
        for d in (1, 7, 2, 6, 3, 5, 4):
            third_copy(d, h).wait_recv()
            total = total + r3[d, rows]
        return total

    for h in (1, 0):
        for d in (4, 3, 5, 2, 6, 1, 7):
            third_copy(d, h).start()

    pltpu.make_async_copy(r1, r1, swap_sem.at[16]).wait()
    pltpu.make_async_copy(r1.at[:15], r1.at[:15], sem1.at[0]).wait()

    @pl.when(jnp.logical_not(home))
    def _():
        pltpu.make_async_copy(r1.at[0], r1.at[0], sem1.at[0]).wait()

    total = z_sum(1)
    for i in range(4):
        q[i] = total[4 * i : 4 * i + 4]

    def out_copy(dx, core):
        cx = (x + dx) % 4
        copy = pltpu.make_async_remote_copy(
            src_ref=q.at[cx], dst_ref=r5.at[2 * x + c], send_sem=sem5.at[0], recv_sem=sem5.at[1],
            device_id=(chip_at(y, cx), core), device_id_type=MESH,
        )
        return copy, jnp.logical_and(dx == 0, c == core)

    for dx in (2, 1, 3, 0):
        for core in range(2):
            copy, mine = out_copy(dx, core)
            if dx:
                copy.start()
            else:

                @pl.when(jnp.logical_not(mine))
                def _():
                    copy.start()

                @pl.when(mine)
                def _():
                    pltpu.make_async_copy(q.at[x], r5.at[2 * x + c], sem5.at[1]).start()

    total = z_sum(0)
    for i in range(2):
        t[i] = total[8 * i : 8 * i + 8]

    def band_copy(j, core):
        row = target(0, j)[1]
        chip = chip_at(2 * c + row, x)
        copy = pltpu.make_async_remote_copy(
            src_ref=t.at[row], dst_ref=r6.at[y], send_sem=sem6.at[0], recv_sem=sem6.at[1],
            device_id=(chip, core), device_id_type=MESH,
        )
        return copy, jnp.logical_and(chip == s, c == core)

    for j in range(2):
        for core in range(2):
            copy, mine = band_copy(j, core)
            if not j:
                copy.start()
            else:

                @pl.when(jnp.logical_not(mine))
                def _():
                    copy.start()

                @pl.when(mine)
                def _():
                    pltpu.make_async_copy(t.at[y % 2], r6.at[y], sem6.at[1]).start()

    for h in range(2):
        rows = pl.ds(16 * h, 16)
        pltpu.make_async_copy(r3.at[1:, rows], r3.at[1:, rows], sem3.at[h, 0]).wait()
    lane, rho = iota((8, 256), 1), iota((8, 256), 0)
    angle = (rho % 4) * (lane + 256 * c) + 128 * (rho // 4)
    turn_real, turn_imag = cos512(angle), cos512(angle - 128)
    side = jnp.where(rho < 4, -1.0, 1.0)

    pltpu.make_async_copy(r5, r5, sem5.at[1]).wait()
    mask = iota((8, 128), 0) == iota((8, 128), 1) % 8
    columns = []
    for j in range(8):
        rows = r5[j]
        columns.append(jnp.concatenate([jnp.where(mask, rows[i : i + 1], 0.0) for i in range(4)], axis=0))
    moved = dot3(jnp.concatenate(columns, axis=1), back_high[...], back_low[...])
    reals, imags = [], []
    for i in range(4):
        tile = moved[8 * i : 8 * i + 8]
        sine = tile[:, 128:]
        pair = tile[:, :128] + side[:, :128] * jnp.concatenate((sine[4:], sine[:4]), axis=0)
        twice = jnp.concatenate((pair, pair), axis=1)
        reals.append(jnp.sum(twice * turn_real, axis=0, keepdims=True))
        imags.append(jnp.sum(twice * turn_imag, axis=0, keepdims=True))
    out[2] = jnp.concatenate(reals, axis=0)
    out[3] = jnp.concatenate(imags, axis=0)

    pltpu.make_async_copy(r6, r6, sem6.at[1]).wait()
    halves = [jnp.concatenate((r6[2 * i], r6[2 * i + 1]), axis=1) for i in range(2)]
    sums = dot3(jnp.concatenate(halves, axis=0), e_high[...], e_low[...])
    sign = (1 - 2 * (lane % 2)).astype(F32)
    cosine = sums[:8, :256] + sign * sums[8:, :256]
    sine = sums[:8, 256:] + sign * sums[8:, 256:]
    result = cosine - side * jnp.concatenate((sine[4:], sine[:4]), axis=0)
    out[0] = result[:4]
    out[1] = result[4:]

    pltpu.make_async_copy(r5.at[:7], r5.at[:7], sem5.at[0]).wait()
    pltpu.make_async_copy(r6.at[:3], r6.at[:3], sem6.at[0]).wait()

    @pl.when(jnp.logical_not(home))
    def _():
        pltpu.make_async_copy(r6.at[0], r6.at[0], sem6.at[0]).wait()


def per_device(frames, aperture, upper_pixels, lower_pixels):
    tiled = frames.reshape(128, 4, 4, 128).transpose(0, 2, 1, 3).reshape(128, 2, 8, 128)
    operands = (tiled, aperture.reshape(1, 256), upper_pixels.T, lower_pixels.T)
    hbm = pl.BlockSpec(memory_space=pltpu.HBM)
    dma = pltpu.SemaphoreType.DMA
    both = pl.pallas_call(
        kernel,
        out_shape=pltpu.VMEM((4, 4, 256), F32),
        in_specs=[hbm] * 4,
        out_specs=pl.BlockSpec(memory_space=pltpu.VMEM),
        scratch_shapes=[
            pltpu.VMEM((128, 2, 8, 128), F32),
            pltpu.VMEM((1, 256), jnp.int32),
            pltpu.VMEM((64, 128), jnp.int32),
            pltpu.VMEM((64, 128), jnp.int32),
            pltpu.VMEM((128, 128), F32),
            pltpu.VMEM((2, 2, 4, 2, 4, 16, 128), F32),
            pltpu.VMEM((16, 4, 16, 128), F32),
            pltpu.VMEM((16, 4, 16, 128), F32),
            pltpu.VMEM((8, 32, 128), F32),
            pltpu.VMEM((8, 32, 128), F32),
            pltpu.VMEM((4, 4, 128), F32),
            pltpu.VMEM((8, 4, 128), F32),
            pltpu.VMEM((2, 8, 128), F32),
            pltpu.VMEM((4, 8, 128), F32),
            pltpu.VMEM((256, 512), BF16),
            pltpu.VMEM((256, 512), BF16),
            pltpu.VMEM((1024, 256), BF16),
            pltpu.VMEM((1024, 256), BF16),
            dma((3 + LOADS,)), dma((17,)), dma((2,)), dma((2, 8)), dma((2,)), dma((2,)),
        ],
        compiler_params=pltpu.CompilerParams(
            collective_id=0, has_side_effects=True, vmem_limit_bytes=32 * 1024 * 1024
        ),
    )(*[pltpu.with_memory_space_constraint(operand, pltpu.HBM) for operand in operands])
    return both[:2], both[2:].transpose(0, 2, 1)


def solution(mesh):
    placed = (P("det", "scan", None), P(), P(), P())
    return jax.shard_map(
        per_device,
        mesh=mesh,
        in_specs=placed,
        out_specs=(P(None, "scan", "det"), P(None, "det", "scan")),
        check_vma=False,
    )
```

```python
import math

import jax
import jax.numpy as jnp
from jax import lax
from jax.experimental import pallas as pl
from jax.experimental.pallas import tpu as pltpu
from jax.sharding import PartitionSpec as P

MESH = pl.DeviceIdType.MESH
F32 = jnp.float32
BF16 = jnp.bfloat16
UNIT = 2.0 * math.pi / 512
SIN = (-1.0 / 6, 1.0 / 120, -1.0 / 5040, 1.0 / 362880, -1.0 / 39916800)


def cos512(m):
    m = m & 511
    t = (128 - jnp.minimum(m, 512 - m)).astype(F32) * UNIT
    t2 = t * t
    poly = jnp.full_like(t, SIN[-1])
    for coefficient in SIN[-2::-1]:
        poly = poly * t2 + coefficient
    return t + t * (t2 * poly)


def split(a):
    high = a.astype(BF16)
    return high, (a - high.astype(F32)).astype(BF16)


def dot(a, b):
    return jnp.dot(a, b, preferred_element_type=F32)


def dot3(a, b_high, b_low):
    rows = a.shape[0]
    a_high, a_low = split(a)
    both = dot(jnp.concatenate((a_high, a_low), axis=0), b_high)
    return both[:rows] + both[rows:] + dot(a_high, b_low)


def iota(shape, dimension):
    return lax.broadcasted_iota(jnp.int32, shape, dimension)


LOADS = 4


def kernel(
    frames, aperture, upper, lower,
    out,
    f, ap, up, lo, w, a, b, r1, zs, r3, q, r5, t, r6, e_high, e_low, back_high, back_low,
    load_sem, swap_sem, sem1, sem3, sem5, sem6,
):
    s = lax.axis_index("scan")
    c = lax.axis_index("det")
    y, z, x = s // 32, (s // 4) % 8, s % 4
    me = y * 4 + x
    home = y // 2 == c

    def chip_at(cy, cx):
        return cy * 32 + z * 4 + cx

    first_row = jnp.where(home, 1 - y % 2, y % 2)
    TARGETS = [(dx, j, k) for k in range(2) for j in range(2) for dx in (2, 1, 3, 0)]

    def target(dx, j):
        return (x + dx) % 4, first_row * (1 - j) + (1 - first_row) * j

    def z_peer(d):
        return s + ((z + d) % 8 - z) * 4

    loads = [
        pltpu.make_async_copy(upper, up, load_sem.at[0]),
        pltpu.make_async_copy(lower, lo, load_sem.at[1]),
        pltpu.make_async_copy(aperture, ap, load_sem.at[2]),
    ]
    for i in range(LOADS):
        pixels = pl.ds(i * (128 // LOADS), 128 // LOADS)
        loads.append(pltpu.make_async_copy(frames.at[pixels], f.at[pixels], load_sem.at[3 + i]))
    for load in loads:
        load.start()

    barrier = pltpu.get_barrier_semaphore()

    def greet(scan, det):
        pl.semaphore_signal(barrier, inc=1, device_id=(scan, det), device_id_type=MESH)

    for d in (4, 3, 5, 2, 6, 1, 7):
        greet(z_peer(d), c)
    for dx in (2, 1, 3, 0):
        for dy in (2, 1, 3, 0):

            @pl.when(jnp.logical_or(jnp.logical_not(home), dx + dy > 0))
            def _():
                greet(chip_at((y + dy) % 4, (x + dx) % 4), y // 2)

        @pl.when(jnp.logical_or(home, dx > 0))
        def _():
            greet(chip_at(y, (x + dx) % 4), 1 - y // 2)

    for load in loads[:3]:
        load.wait()
    pixel = (iota((128, 128), 0) + 128 * c).astype(F32).astype(BF16)
    one, none = jnp.ones((128, 128), BF16), jnp.zeros((128, 128), BF16)

    def row_of(ref, j):
        return jnp.broadcast_to(ref[pl.ds(j, 1), :], (128, 128)).astype(F32).astype(BF16)

    def count(j, total):
        total = total + jnp.where(row_of(up, j) == pixel, one, none)
        return total - jnp.where(row_of(lo, j) == pixel, one, none)

    counts = lax.fori_loop(0, 64, count, none, unroll=4)
    w[...] = (counts.astype(F32) * (64**-0.5 / 512)).T
    tiles = [w[pl.ds(32 * (i % 4) + i // 4, 8, stride=4), :] for i in range(16)]
    inside = jnp.where(c == 0, ap[:, :128], ap[:, 128:]).astype(F32)
    weight = (jnp.concatenate(tiles, axis=0) * inside).astype(BF16)
    weight = jnp.concatenate((weight, weight), axis=1)

    flat = f.reshape(2048, 128)

    def weighted(half):
        for i in range(4):
            rows = [flat[pl.ds(8 * half + 4 * j + i, 128, stride=16), :] for j in range(2)]
            high, low = split(jnp.concatenate(rows, axis=1))
            sums = dot(weight, jnp.concatenate((high, low), axis=0))
            for j in range(2):
                a[half, j, :, :, i] = sums[:, 128 * j : 128 * j + 128].reshape(4, 2, 16, 128)

    for load in loads[3:]:
        load.wait()
    weighted(1 - c)
    weighted(c)

    pl.semaphore_wait(barrier, jnp.where(home, 22, 30))

    def swap_copy(i):
        dx, j, k = TARGETS[i]
        cx, row = target(dx, j)
        far_row = jnp.where(home, y % 2, 1 - y % 2) * (1 - j) + jnp.where(home, 1 - y % 2, y % 2) * j
        return pltpu.make_async_remote_copy(
            src_ref=a.at[1 - c, far_row, cx, (1 - c + k) % 2], dst_ref=b.at[i],
            send_sem=swap_sem.at[16], recv_sem=swap_sem.at[i], device_id=(s, 1 - c), device_id_type=MESH,
        )

    for i in range(16):
        swap_copy(i).start()

    def first_copy(i):
        dx, j, k = TARGETS[i]
        cx, row = target(dx, j)
        chip = chip_at(2 * c + row, cx)
        copy = pltpu.make_async_remote_copy(
            src_ref=b.at[i], dst_ref=r1.at[me], send_sem=sem1.at[0], recv_sem=sem1.at[1],
            device_id=(chip, (c + k) % 2), device_id_type=MESH,
        )
        return copy, chip == s

    for i, (dx, j, k) in enumerate(TARGETS):
        cx, row = target(dx, j)
        swap_copy(i).wait_recv()
        b[i] = b[i] + a[c, row, cx, (c + k) % 2]
        copy, mine = first_copy(i)
        if dx or not j or k:
            copy.start()
        else:

            @pl.when(jnp.logical_not(mine))
            def _():
                copy.start()

            @pl.when(mine)
            def _():
                pltpu.make_async_copy(b.at[i], r1.at[me], sem1.at[1]).start()

    row, column = iota((64, 512), 0), iota((64, 512), 1)
    chip = (column // 128) * 32 + 4 * z + (column // 32) % 4
    place = 4 * chip + (column // 8) % 4
    same = row // 8 == column % 8
    lefts = []
    for i in range(2):
        block = (2 * c + i) * 32 + x + 4 * (row // 8)
        left = cos512((4 * block + row % 4) * place + 32 * (row % 8 - row % 4))
        lefts.append(split(jnp.where(same, left, 0.0)))

    frequency = iota((256, 512), 1)
    wide = frequency % 256 + 256 * c
    table_high, table_low = split(cos512(wide * iota((256, 512), 0) - 128 * (frequency // 256)))
    e_high[...] = table_high
    e_low[...] = table_low

    n, source = iota((1024, 256), 1), iota((1024, 256), 0)
    source_block = ((source // 64) % 4) * 32 + source // 256 + 4 * ((source // 8) % 8)
    table_high, table_low = split(cos512(4 * source_block * (n % 128) - 128 * (n // 128)))
    back_high[...] = table_high
    back_low[...] = table_low

    pltpu.make_async_copy(r1, r1, sem1.at[1]).wait()
    parts = []
    for i in range(2):
        right = jnp.concatenate([r1[k, :, 8 * i : 8 * i + 8].reshape(32, 128) for k in range(16)], axis=0)
        right_high, right_low = split(right)
        left_high, left_low = lefts[i]
        both = dot(jnp.concatenate((left_high, left_low), axis=0), right_high)
        parts.append((both[:64] + both[64:]) + dot(left_high, right_low))

    turned = jnp.concatenate(parts, axis=0).T
    for i in range(8):
        zs[i, :8] = parts[0][8 * i : 8 * i + 8]
        zs[i, 8:16] = parts[1][8 * i : 8 * i + 8]
        zs[i, 16:] = turned[16 * i : 16 * i + 16]

    def third_copy(d, h):
        rows = pl.ds(16 * h, 16)
        return pltpu.make_async_remote_copy(
            src_ref=zs.at[(z + d) % 8, rows], dst_ref=r3.at[d, rows],
            send_sem=sem3.at[h, 0], recv_sem=sem3.at[h, d],
            device_id=(z_peer(d), c), device_id_type=MESH,
        )

    def z_sum(h):
        rows = pl.ds(16 * h, 16)
        total = zs[z, rows]
        for d in (1, 7, 2, 6, 3, 5, 4):
            third_copy(d, h).wait_recv()
            total = total + r3[d, rows]
        return total

    for h in (1, 0):
        for d in (4, 3, 5, 2, 6, 1, 7):
            third_copy(d, h).start()

    pltpu.make_async_copy(r1, r1, swap_sem.at[16]).wait()
    pltpu.make_async_copy(r1.at[:15], r1.at[:15], sem1.at[0]).wait()

    @pl.when(jnp.logical_not(home))
    def _():
        pltpu.make_async_copy(r1.at[0], r1.at[0], sem1.at[0]).wait()

    total = z_sum(1)
    for i in range(4):
        q[i] = total[4 * i : 4 * i + 4]

    def out_copy(dx, core):
        cx = (x + dx) % 4
        copy = pltpu.make_async_remote_copy(
            src_ref=q.at[cx], dst_ref=r5.at[2 * x + c], send_sem=sem5.at[0], recv_sem=sem5.at[1],
            device_id=(chip_at(y, cx), core), device_id_type=MESH,
        )
        return copy, jnp.logical_and(dx == 0, c == core)

    for dx in (2, 1, 3, 0):
        for core in range(2):
            copy, mine = out_copy(dx, core)
            if dx:
                copy.start()
            else:

                @pl.when(jnp.logical_not(mine))
                def _():
                    copy.start()

                @pl.when(mine)
                def _():
                    pltpu.make_async_copy(q.at[x], r5.at[2 * x + c], sem5.at[1]).start()

    total = z_sum(0)
    for i in range(2):
        t[i] = total[8 * i : 8 * i + 8]

    def band_copy(j, core):
        row = target(0, j)[1]
        chip = chip_at(2 * c + row, x)
        copy = pltpu.make_async_remote_copy(
            src_ref=t.at[row], dst_ref=r6.at[y], send_sem=sem6.at[0], recv_sem=sem6.at[1],
            device_id=(chip, core), device_id_type=MESH,
        )
        return copy, jnp.logical_and(chip == s, c == core)

    for j in range(2):
        for core in range(2):
            copy, mine = band_copy(j, core)
            if not j:
                copy.start()
            else:

                @pl.when(jnp.logical_not(mine))
                def _():
                    copy.start()

                @pl.when(mine)
                def _():
                    pltpu.make_async_copy(t.at[y % 2], r6.at[y], sem6.at[1]).start()

    for h in range(2):
        rows = pl.ds(16 * h, 16)
        pltpu.make_async_copy(r3.at[1:, rows], r3.at[1:, rows], sem3.at[h, 0]).wait()
    lane, rho = iota((8, 256), 1), iota((8, 256), 0)
    angle = (rho % 4) * (lane + 256 * c) + 128 * (rho // 4)
    turn_real, turn_imag = cos512(angle), cos512(angle - 128)
    side = jnp.where(rho < 4, -1.0, 1.0)

    pltpu.make_async_copy(r5, r5, sem5.at[1]).wait()
    mask = iota((8, 128), 0) == iota((8, 128), 1) % 8
    columns = []
    for j in range(8):
        rows = r5[j]
        columns.append(jnp.concatenate([jnp.where(mask, rows[i : i + 1], 0.0) for i in range(4)], axis=0))
    moved = dot3(jnp.concatenate(columns, axis=1), back_high[...], back_low[...])
    reals, imags = [], []
    for i in range(4):
        tile = moved[8 * i : 8 * i + 8]
        sine = tile[:, 128:]
        pair = tile[:, :128] + side[:, :128] * jnp.concatenate((sine[4:], sine[:4]), axis=0)
        twice = jnp.concatenate((pair, pair), axis=1)
        reals.append(jnp.sum(twice * turn_real, axis=0, keepdims=True))
        imags.append(jnp.sum(twice * turn_imag, axis=0, keepdims=True))
    out[2] = jnp.concatenate(reals, axis=0)
    out[3] = jnp.concatenate(imags, axis=0)

    pltpu.make_async_copy(r6, r6, sem6.at[1]).wait()
    halves = [jnp.concatenate((r6[2 * i], r6[2 * i + 1]), axis=1) for i in range(2)]
    sums = dot3(jnp.concatenate(halves, axis=0), e_high[...], e_low[...])
    sign = (1 - 2 * (lane % 2)).astype(F32)
    cosine = sums[:8, :256] + sign * sums[8:, :256]
    sine = sums[:8, 256:] + sign * sums[8:, 256:]
    result = cosine - side * jnp.concatenate((sine[4:], sine[:4]), axis=0)
    out[0] = result[:4]
    out[1] = result[4:]

    pltpu.make_async_copy(r5.at[:7], r5.at[:7], sem5.at[0]).wait()
    pltpu.make_async_copy(r6.at[:3], r6.at[:3], sem6.at[0]).wait()

    @pl.when(jnp.logical_not(home))
    def _():
        pltpu.make_async_copy(r6.at[0], r6.at[0], sem6.at[0]).wait()


def per_device(frames, aperture, upper_pixels, lower_pixels):
    tiled = frames.reshape(128, 4, 4, 128).transpose(0, 2, 1, 3).reshape(128, 2, 8, 128)
    operands = (tiled, aperture.reshape(1, 256), upper_pixels.T, lower_pixels.T)
    hbm = pl.BlockSpec(memory_space=pltpu.HBM)
    dma = pltpu.SemaphoreType.DMA
    both = pl.pallas_call(
        kernel,
        out_shape=pltpu.VMEM((4, 4, 256), F32),
        in_specs=[hbm] * 4,
        out_specs=pl.BlockSpec(memory_space=pltpu.VMEM),
        scratch_shapes=[
            pltpu.VMEM((128, 2, 8, 128), F32),
            pltpu.VMEM((1, 256), jnp.int32),
            pltpu.VMEM((64, 128), jnp.int32),
            pltpu.VMEM((64, 128), jnp.int32),
            pltpu.VMEM((128, 128), F32),
            pltpu.VMEM((2, 2, 4, 2, 4, 16, 128), F32),
            pltpu.VMEM((16, 4, 16, 128), F32),
            pltpu.VMEM((16, 4, 16, 128), F32),
            pltpu.VMEM((8, 32, 128), F32),
            pltpu.VMEM((8, 32, 128), F32),
            pltpu.VMEM((4, 4, 128), F32),
            pltpu.VMEM((8, 4, 128), F32),
            pltpu.VMEM((2, 8, 128), F32),
            pltpu.VMEM((4, 8, 128), F32),
            pltpu.VMEM((256, 512), BF16),
            pltpu.VMEM((256, 512), BF16),
            pltpu.VMEM((1024, 256), BF16),
            pltpu.VMEM((1024, 256), BF16),
            dma((3 + LOADS,)), dma((17,)), dma((2,)), dma((2, 8)), dma((2,)), dma((2,)),
        ],
        compiler_params=pltpu.CompilerParams(
            collective_id=0, has_side_effects=True, vmem_limit_bytes=32 * 1024 * 1024
        ),
    )(*[pltpu.with_memory_space_constraint(operand, pltpu.HBM) for operand in operands])
    return both[:2], both[2:].transpose(0, 2, 1)


def solution(mesh):
    placed = (P("det", "scan", None), P(), P(), P())
    return jax.shard_map(
        per_device,
        mesh=mesh,
        in_specs=placed,
        out_specs=(P(None, "scan", "det"), P(None, "det", "scan")),
        check_vma=False,
    )
```

```python
import math

import jax
import jax.numpy as jnp
from jax import lax
from jax.experimental import pallas as pl
from jax.experimental.pallas import tpu as pltpu
from jax.sharding import PartitionSpec as P

MESH = pl.DeviceIdType.MESH
F32 = jnp.float32
BF16 = jnp.bfloat16
UNIT = 2.0 * math.pi / 512
SIN = (-1.0 / 6, 1.0 / 120, -1.0 / 5040, 1.0 / 362880, -1.0 / 39916800)


def cos512(m):
    m = m & 511
    t = (128 - jnp.minimum(m, 512 - m)).astype(F32) * UNIT
    t2 = t * t
    poly = jnp.full_like(t, SIN[-1])
    for coefficient in SIN[-2::-1]:
        poly = poly * t2 + coefficient
    return t + t * (t2 * poly)


def split(a):
    high = a.astype(BF16)
    return high, (a - high.astype(F32)).astype(BF16)


def dot(a, b):
    return jnp.dot(a, b, preferred_element_type=F32)


def dot3(a, b_high, b_low):
    rows = a.shape[0]
    a_high, a_low = split(a)
    both = dot(jnp.concatenate((a_high, a_low), axis=0), b_high)
    return both[:rows] + both[rows:] + dot(a_high, b_low)


def iota(shape, dimension):
    return lax.broadcasted_iota(jnp.int32, shape, dimension)


LOADS = 4


def kernel(
    frames, aperture, upper, lower,
    out,
    f, ap, up, lo, w, a, b, r1, zs, r3, q, r5, t, r6, e_high, e_low, back_high, back_low,
    load_sem, swap_sem, sem1, sem3, sem5, sem6,
):
    s = lax.axis_index("scan")
    c = lax.axis_index("det")
    y, z, x = s // 32, (s // 4) % 8, s % 4
    me = y * 4 + x
    home = y // 2 == c

    def chip_at(cy, cx):
        return cy * 32 + z * 4 + cx

    first_row = jnp.where(home, 1 - y % 2, y % 2)
    TARGETS = [(dx, j, k) for k in range(2) for j in range(2) for dx in (2, 1, 3, 0)]

    def target(dx, j):
        return (x + dx) % 4, first_row * (1 - j) + (1 - first_row) * j

    def z_peer(d):
        return s + ((z + d) % 8 - z) * 4

    loads = [
        pltpu.make_async_copy(upper, up, load_sem.at[0]),
        pltpu.make_async_copy(lower, lo, load_sem.at[1]),
        pltpu.make_async_copy(aperture, ap, load_sem.at[2]),
    ]
    for i in range(LOADS):
        pixels = pl.ds(i * (128 // LOADS), 128 // LOADS)
        loads.append(pltpu.make_async_copy(frames.at[pixels], f.at[pixels], load_sem.at[3 + i]))
    for load in loads:
        load.start()

    barrier = pltpu.get_barrier_semaphore()

    def greet(scan, det):
        pl.semaphore_signal(barrier, inc=1, device_id=(scan, det), device_id_type=MESH)

    for d in (4, 3, 5, 2, 6, 1, 7):
        greet(z_peer(d), c)
    for dx in (2, 1, 3, 0):
        for dy in (2, 1, 3, 0):

            @pl.when(jnp.logical_or(jnp.logical_not(home), dx + dy > 0))
            def _():
                greet(chip_at((y + dy) % 4, (x + dx) % 4), y // 2)

        @pl.when(jnp.logical_or(home, dx > 0))
        def _():
            greet(chip_at(y, (x + dx) % 4), 1 - y // 2)

    for load in loads[:3]:
        load.wait()
    pixel = (iota((128, 128), 0) + 128 * c).astype(F32).astype(BF16)
    one, none = jnp.ones((128, 128), BF16), jnp.zeros((128, 128), BF16)

    def row_of(ref, j):
        return jnp.broadcast_to(ref[pl.ds(j, 1), :], (128, 128)).astype(F32).astype(BF16)

    def count(j, total):
        total = total + jnp.where(row_of(up, j) == pixel, one, none)
        return total - jnp.where(row_of(lo, j) == pixel, one, none)

    counts = lax.fori_loop(0, 64, count, none, unroll=4)
    w[...] = (counts.astype(F32) * (64**-0.5 / 512)).T
    tiles = [w[pl.ds(32 * (i % 4) + i // 4, 8, stride=4), :] for i in range(16)]
    inside = jnp.where(c == 0, ap[:, :128], ap[:, 128:]).astype(F32)
    weight = (jnp.concatenate(tiles, axis=0) * inside).astype(BF16)
    weight = jnp.concatenate((weight, weight), axis=1)

    flat = f.reshape(2048, 128)

    def weighted(half):
        for i in range(4):
            rows = [flat[pl.ds(8 * half + 4 * j + i, 128, stride=16), :] for j in range(2)]
            high, low = split(jnp.concatenate(rows, axis=1))
            sums = dot(weight, jnp.concatenate((high, low), axis=0))
            for j in range(2):
                a[half, j, :, :, i] = sums[:, 128 * j : 128 * j + 128].reshape(4, 2, 16, 128)

    for load in loads[3:]:
        load.wait()
    weighted(1 - c)
    weighted(c)

    pl.semaphore_wait(barrier, jnp.where(home, 22, 30))

    def swap_copy(i):
        dx, j, k = TARGETS[i]
        cx, row = target(dx, j)
        far_row = jnp.where(home, y % 2, 1 - y % 2) * (1 - j) + jnp.where(home, 1 - y % 2, y % 2) * j
        return pltpu.make_async_remote_copy(
            src_ref=a.at[1 - c, far_row, cx, (1 - c + k) % 2], dst_ref=b.at[i],
            send_sem=swap_sem.at[16], recv_sem=swap_sem.at[i], device_id=(s, 1 - c), device_id_type=MESH,
        )

    for i in range(16):
        swap_copy(i).start()

    def first_copy(i):
        dx, j, k = TARGETS[i]
        cx, row = target(dx, j)
        chip = chip_at(2 * c + row, cx)
        copy = pltpu.make_async_remote_copy(
            src_ref=b.at[i], dst_ref=r1.at[me], send_sem=sem1.at[0], recv_sem=sem1.at[1],
            device_id=(chip, (c + k) % 2), device_id_type=MESH,
        )
        return copy, chip == s

    for i, (dx, j, k) in enumerate(TARGETS):
        cx, row = target(dx, j)
        swap_copy(i).wait_recv()
        b[i] = b[i] + a[c, row, cx, (c + k) % 2]
        copy, mine = first_copy(i)
        if dx or k:
            copy.start()
        else:

            @pl.when(jnp.logical_not(mine))
            def _():
                copy.start()

            @pl.when(mine)
            def _():
                pltpu.make_async_copy(b.at[i], r1.at[me], sem1.at[1]).start()

    row, column = iota((64, 512), 0), iota((64, 512), 1)
    chip = (column // 128) * 32 + 4 * z + (column // 32) % 4
    place = 4 * chip + (column // 8) % 4
    same = row // 8 == column % 8
    lefts = []
    for i in range(2):
        block = (2 * c + i) * 32 + x + 4 * (row // 8)
        left = cos512((4 * block + row % 4) * place + 32 * (row % 8 - row % 4))
        lefts.append(split(jnp.where(same, left, 0.0)))

    frequency = iota((256, 512), 1)
    wide = frequency % 256 + 256 * c
    table_high, table_low = split(cos512(wide * iota((256, 512), 0) - 128 * (frequency // 256)))
    e_high[...] = table_high
    e_low[...] = table_low

    n, source = iota((1024, 256), 1), iota((1024, 256), 0)
    source_block = ((source // 64) % 4) * 32 + source // 256 + 4 * ((source // 8) % 8)
    table_high, table_low = split(cos512(4 * source_block * (n % 128) - 128 * (n // 128)))
    back_high[...] = table_high
    back_low[...] = table_low

    pltpu.make_async_copy(r1, r1, sem1.at[1]).wait()
    parts = []
    for i in range(2):
        right = jnp.concatenate([r1[k, :, 8 * i : 8 * i + 8].reshape(32, 128) for k in range(16)], axis=0)
        right_high, right_low = split(right)
        left_high, left_low = lefts[i]
        both = dot(jnp.concatenate((left_high, left_low), axis=0), right_high)
        parts.append((both[:64] + both[64:]) + dot(left_high, right_low))

    turned = jnp.concatenate(parts, axis=0).T
    for i in range(8):
        zs[i, :8] = parts[0][8 * i : 8 * i + 8]
        zs[i, 8:16] = parts[1][8 * i : 8 * i + 8]
        zs[i, 16:] = turned[16 * i : 16 * i + 16]

    def third_copy(d):
        return pltpu.make_async_remote_copy(
            src_ref=zs.at[(z + d) % 8], dst_ref=r3.at[d], send_sem=sem3.at[0], recv_sem=sem3.at[d],
            device_id=(z_peer(d), c), device_id_type=MESH,
        )

    for d in (4, 5, 3, 6, 2, 7, 1):
        third_copy(d).start()

    pltpu.make_async_copy(r1, r1, swap_sem.at[16]).wait()
    pltpu.make_async_copy(r1.at[:15], r1.at[:15], sem1.at[0]).wait()

    @pl.when(jnp.logical_not(home))
    def _():
        pltpu.make_async_copy(r1.at[0], r1.at[0], sem1.at[0]).wait()

    total = zs[z]
    for d in (1, 7, 2, 6, 3, 5, 4):
        third_copy(d).wait_recv()
        total = total + r3[d]
    for i in range(2):
        t[i] = total[8 * i : 8 * i + 8]

    def band_copy(j, core):
        row = target(0, j)[1]
        chip = chip_at(2 * c + row, x)
        copy = pltpu.make_async_remote_copy(
            src_ref=t.at[row], dst_ref=r6.at[y], send_sem=sem6.at[0], recv_sem=sem6.at[1],
            device_id=(chip, core), device_id_type=MESH,
        )
        return copy, jnp.logical_and(chip == s, c == core)

    for j in range(2):
        for core in (1, 0):
            copy, mine = band_copy(j, core)

            @pl.when(jnp.logical_not(mine))
            def _():
                copy.start()

            @pl.when(mine)
            def _():
                pltpu.make_async_copy(t.at[y % 2], r6.at[y], sem6.at[1]).start()

    for i in range(4):
        q[i] = total[16 + 4 * i : 20 + 4 * i]

    def out_copy(dx, core):
        cx = (x + dx) % 4
        copy = pltpu.make_async_remote_copy(
            src_ref=q.at[cx], dst_ref=r5.at[2 * x + c], send_sem=sem5.at[0], recv_sem=sem5.at[1],
            device_id=(chip_at(y, cx), core), device_id_type=MESH,
        )
        return copy, jnp.logical_and(dx == 0, c == core)

    for dx in (2, 1, 3, 0):
        for core in (1, 0):
            copy, mine = out_copy(dx, core)
            if dx:
                copy.start()
            else:

                @pl.when(jnp.logical_not(mine))
                def _():
                    copy.start()

                @pl.when(mine)
                def _():
                    pltpu.make_async_copy(q.at[x], r5.at[2 * x + c], sem5.at[1]).start()

    pltpu.make_async_copy(r3.at[1:], r3.at[1:], sem3.at[0]).wait()
    lane, rho = iota((8, 256), 1), iota((8, 256), 0)
    angle = (rho % 4) * (lane + 256 * c) + 128 * (rho // 4)
    turn_real, turn_imag = cos512(angle), cos512(angle - 128)
    side = jnp.where(rho < 4, -1.0, 1.0)

    pltpu.make_async_copy(r5, r5, sem5.at[1]).wait()
    mask = iota((8, 128), 0) == iota((8, 128), 1) % 8
    columns = []
    for j in range(8):
        rows = r5[j]
        columns.append(jnp.concatenate([jnp.where(mask, rows[i : i + 1], 0.0) for i in range(4)], axis=0))
    moved = dot3(jnp.concatenate(columns, axis=1), back_high[...], back_low[...])
    reals, imags = [], []
    for i in range(4):
        tile = moved[8 * i : 8 * i + 8]
        sine = tile[:, 128:]
        pair = tile[:, :128] + side[:, :128] * jnp.concatenate((sine[4:], sine[:4]), axis=0)
        twice = jnp.concatenate((pair, pair), axis=1)
        reals.append(jnp.sum(twice * turn_real, axis=0, keepdims=True))
        imags.append(jnp.sum(twice * turn_imag, axis=0, keepdims=True))
    out[2] = jnp.concatenate(reals, axis=0)
    out[3] = jnp.concatenate(imags, axis=0)

    pltpu.make_async_copy(r6, r6, sem6.at[1]).wait()
    halves = [jnp.concatenate((r6[2 * i], r6[2 * i + 1]), axis=1) for i in range(2)]
    sums = dot3(jnp.concatenate(halves, axis=0), e_high[...], e_low[...])
    sign = (1 - 2 * (lane % 2)).astype(F32)
    cosine = sums[:8, :256] + sign * sums[8:, :256]
    sine = sums[:8, 256:] + sign * sums[8:, 256:]
    result = cosine - side * jnp.concatenate((sine[4:], sine[:4]), axis=0)
    out[0] = result[:4]
    out[1] = result[4:]

    pltpu.make_async_copy(r5.at[:7], r5.at[:7], sem5.at[0]).wait()
    pltpu.make_async_copy(r6.at[:3], r6.at[:3], sem6.at[0]).wait()

    @pl.when(jnp.logical_not(home))
    def _():
        pltpu.make_async_copy(r6.at[0], r6.at[0], sem6.at[0]).wait()


def per_device(frames, aperture, upper_pixels, lower_pixels):
    tiled = frames.reshape(128, 4, 4, 128).transpose(0, 2, 1, 3).reshape(128, 2, 8, 128)
    operands = (tiled, aperture.reshape(1, 256), upper_pixels.T, lower_pixels.T)
    hbm = pl.BlockSpec(memory_space=pltpu.HBM)
    dma = pltpu.SemaphoreType.DMA
    both = pl.pallas_call(
        kernel,
        out_shape=pltpu.VMEM((4, 4, 256), F32),
        in_specs=[hbm] * 4,
        out_specs=pl.BlockSpec(memory_space=pltpu.VMEM),
        scratch_shapes=[
            pltpu.VMEM((128, 2, 8, 128), F32),
            pltpu.VMEM((1, 256), jnp.int32),
            pltpu.VMEM((64, 128), jnp.int32),
            pltpu.VMEM((64, 128), jnp.int32),
            pltpu.VMEM((128, 128), F32),
            pltpu.VMEM((2, 2, 4, 2, 4, 16, 128), F32),
            pltpu.VMEM((16, 4, 16, 128), F32),
            pltpu.VMEM((16, 4, 16, 128), F32),
            pltpu.VMEM((8, 32, 128), F32),
            pltpu.VMEM((8, 32, 128), F32),
            pltpu.VMEM((4, 4, 128), F32),
            pltpu.VMEM((8, 4, 128), F32),
            pltpu.VMEM((2, 8, 128), F32),
            pltpu.VMEM((4, 8, 128), F32),
            pltpu.VMEM((256, 512), BF16),
            pltpu.VMEM((256, 512), BF16),
            pltpu.VMEM((1024, 256), BF16),
            pltpu.VMEM((1024, 256), BF16),
            dma((3 + LOADS,)), dma((17,)), dma((2,)), dma((8,)), dma((2,)), dma((2,)),
        ],
        compiler_params=pltpu.CompilerParams(
            collective_id=0, has_side_effects=True, vmem_limit_bytes=32 * 1024 * 1024
        ),
    )(*[pltpu.with_memory_space_constraint(operand, pltpu.HBM) for operand in operands])
    return both[:2], both[2:].transpose(0, 2, 1)


def solution(mesh):
    placed = (P("det", "scan", None), P(), P(), P())
    return jax.shard_map(
        per_device,
        mesh=mesh,
        in_specs=placed,
        out_specs=(P(None, "scan", "det"), P(None, "det", "scan")),
        check_vma=False,
    )
```

```python
import math

import jax
import jax.numpy as jnp
from jax import lax
from jax.experimental import pallas as pl
from jax.experimental.pallas import tpu as pltpu
from jax.sharding import PartitionSpec as P

MESH = pl.DeviceIdType.MESH
F32 = jnp.float32
BF16 = jnp.bfloat16
UNIT = 2.0 * math.pi / 512
SIN = (-1.0 / 6, 1.0 / 120, -1.0 / 5040, 1.0 / 362880, -1.0 / 39916800)


def cos512(m):
    m = m & 511
    t = (128 - jnp.minimum(m, 512 - m)).astype(F32) * UNIT
    t2 = t * t
    poly = jnp.full_like(t, SIN[-1])
    for coefficient in SIN[-2::-1]:
        poly = poly * t2 + coefficient
    return t + t * (t2 * poly)


def split(a):
    high = a.astype(BF16)
    return high, (a - high.astype(F32)).astype(BF16)


def dot(a, b):
    return jnp.dot(a, b, preferred_element_type=F32)


def dot3(a, b_high, b_low):
    rows = a.shape[0]
    a_high, a_low = split(a)
    both = dot(jnp.concatenate((a_high, a_low), axis=0), b_high)
    return both[:rows] + both[rows:] + dot(a_high, b_low)


def iota(shape, dimension):
    return lax.broadcasted_iota(jnp.int32, shape, dimension)


LOADS = 4


def kernel(
    frames, aperture, upper, lower,
    out,
    f, ap, up, lo, w, a, b, r1, zs, r3, q, r5, t, r6, e_high, e_low, back_high, back_low,
    load_sem, swap_sem, sem1, sem3, sem5, sem6,
):
    s = lax.axis_index("scan")
    c = lax.axis_index("det")
    y, z, x = s // 32, (s // 4) % 8, s % 4
    me = y * 4 + x
    home = y // 2 == c

    def chip_at(cy, cx):
        return cy * 32 + z * 4 + cx

    first_row = jnp.where(home, 1 - y % 2, y % 2)
    TARGETS = [(dx, j, k) for k in range(2) for j in range(2) for dx in (2, 1, 3, 0)]

    def target(dx, j):
        return (x + dx) % 4, first_row * (1 - j) + (1 - first_row) * j

    def z_peer(d):
        return s + ((z + d) % 8 - z) * 4

    barrier = pltpu.get_barrier_semaphore()

    def greet(scan, det):
        pl.semaphore_signal(barrier, inc=1, device_id=(scan, det), device_id_type=MESH)

    for d in (4, 3, 5, 2, 6, 1, 7):
        greet(z_peer(d), c)
    for dx in (2, 1, 3, 0):
        for dy in (2, 1, 3, 0):
            if dx or dy:
                greet(chip_at((y + dy) % 4, (x + dx) % 4), y // 2)
        if dx:
            greet(chip_at(y, (x + dx) % 4), 1 - y // 2)
    greet(s, 1 - c)

    loads = [
        pltpu.make_async_copy(upper, up, load_sem.at[0]),
        pltpu.make_async_copy(lower, lo, load_sem.at[1]),
        pltpu.make_async_copy(aperture, ap, load_sem.at[2]),
    ]
    for i in range(LOADS):
        pixels = pl.ds(i * (128 // LOADS), 128 // LOADS)
        loads.append(pltpu.make_async_copy(frames.at[pixels], f.at[pixels], load_sem.at[3 + i]))
    for load in loads:
        load.start()

    for load in loads[:3]:
        load.wait()
    pixel = (iota((128, 128), 0) + 128 * c).astype(F32).astype(BF16)
    one, none = jnp.ones((128, 128), BF16), jnp.zeros((128, 128), BF16)

    def row_of(ref, j):
        return jnp.broadcast_to(ref[pl.ds(j, 1), :], (128, 128)).astype(F32).astype(BF16)

    def count(j, total):
        total = total + jnp.where(row_of(up, j) == pixel, one, none)
        return total - jnp.where(row_of(lo, j) == pixel, one, none)

    counts = lax.fori_loop(0, 64, count, none, unroll=4)
    w[...] = (counts.astype(F32) * (64**-0.5 / 512)).T
    tiles = [w[pl.ds(32 * (i % 4) + i // 4, 8, stride=4), :] for i in range(16)]
    inside = jnp.where(c == 0, ap[:, :128], ap[:, 128:]).astype(F32)
    weight = (jnp.concatenate(tiles, axis=0) * inside).astype(BF16)
    weight = jnp.concatenate((weight, weight), axis=1)

    flat = f.reshape(2048, 128)

    def weighted(half):
        for i in range(4):
            rows = [flat[pl.ds(8 * half + 4 * j + i, 128, stride=16), :] for j in range(2)]
            high, low = split(jnp.concatenate(rows, axis=1))
            sums = dot(weight, jnp.concatenate((high, low), axis=0))
            for j in range(2):
                a[half, j, :, :, i] = sums[:, 128 * j : 128 * j + 128].reshape(4, 2, 16, 128)

    for load in loads[3:]:
        load.wait()
    weighted(1 - c)
    weighted(c)

    pl.semaphore_wait(barrier, jnp.where(home, 22, 30))

    def swap_copy(i):
        dx, j, k = TARGETS[i]
        cx, row = target(dx, j)
        far_row = jnp.where(home, y % 2, 1 - y % 2) * (1 - j) + jnp.where(home, 1 - y % 2, y % 2) * j
        return pltpu.make_async_remote_copy(
            src_ref=a.at[1 - c, far_row, cx, k], dst_ref=b.at[i],
            send_sem=swap_sem.at[16], recv_sem=swap_sem.at[i], device_id=(s, 1 - c), device_id_type=MESH,
        )

    for i in range(16):
        swap_copy(i).start()

    def first_copy(i):
        dx, j, k = TARGETS[i]
        cx, row = target(dx, j)
        chip = chip_at(2 * c + row, cx)
        copy = pltpu.make_async_remote_copy(
            src_ref=b.at[i], dst_ref=r1.at[me], send_sem=sem1.at[0], recv_sem=sem1.at[1],
            device_id=(chip, k), device_id_type=MESH,
        )
        return copy, jnp.logical_and(chip == s, c == k)

    for i, (dx, j, k) in enumerate(TARGETS):
        cx, row = target(dx, j)
        swap_copy(i).wait_recv()
        b[i] = b[i] + a[c, row, cx, k]
        copy, mine = first_copy(i)
        if dx or not j:
            copy.start()
        else:

            @pl.when(jnp.logical_not(mine))
            def _():
                copy.start()

            @pl.when(mine)
            def _():
                pltpu.make_async_copy(b.at[i], r1.at[me], sem1.at[1]).start()

    row, column = iota((64, 512), 0), iota((64, 512), 1)
    chip = (column // 128) * 32 + 4 * z + (column // 32) % 4
    place = 4 * chip + (column // 8) % 4
    same = row // 8 == column % 8
    lefts = []
    for i in range(2):
        block = (2 * c + i) * 32 + x + 4 * (row // 8)
        left = cos512((4 * block + row % 4) * place + 32 * (row % 8 - row % 4))
        lefts.append(split(jnp.where(same, left, 0.0)))

    frequency = iota((256, 512), 1)
    wide = frequency % 256 + 256 * c
    table_high, table_low = split(cos512(wide * iota((256, 512), 0) - 128 * (frequency // 256)))
    e_high[...] = table_high
    e_low[...] = table_low

    n, source = iota((1024, 256), 1), iota((1024, 256), 0)
    source_block = ((source // 64) % 4) * 32 + source // 256 + 4 * ((source // 8) % 8)
    table_high, table_low = split(cos512(4 * source_block * (n % 128) - 128 * (n // 128)))
    back_high[...] = table_high
    back_low[...] = table_low

    pltpu.make_async_copy(r1, r1, sem1.at[1]).wait()
    parts = []
    for i in range(2):
        right = jnp.concatenate([r1[k, :, 8 * i : 8 * i + 8].reshape(32, 128) for k in range(16)], axis=0)
        right_high, right_low = split(right)
        left_high, left_low = lefts[i]
        both = dot(jnp.concatenate((left_high, left_low), axis=0), right_high)
        parts.append((both[:64] + both[64:]) + dot(left_high, right_low))

    turned = jnp.concatenate(parts, axis=0).T
    for i in range(8):
        zs[i, :8] = parts[0][8 * i : 8 * i + 8]
        zs[i, 8:16] = parts[1][8 * i : 8 * i + 8]
        zs[i, 16:] = turned[16 * i : 16 * i + 16]

    def third_copy(d, h):
        rows = pl.ds(16 * h, 16)
        return pltpu.make_async_remote_copy(
            src_ref=zs.at[(z + d) % 8, rows], dst_ref=r3.at[d, rows], send_sem=sem3.at[0], recv_sem=sem3.at[8 * h + d],
            device_id=(z_peer(d), c), device_id_type=MESH,
        )

    def z_sum(h):
        rows = pl.ds(16 * h, 16)
        total = zs[z, rows]
        for d in (1, 7, 2, 6, 3, 5, 4):
            third_copy(d, h).wait_recv()
            total = total + r3[d, rows]
        return total

    for h in range(2):
        for d in (4, 5, 3, 6, 2, 7, 1):
            third_copy(d, h).start()

    pltpu.make_async_copy(r1, r1, swap_sem.at[16]).wait()
    pltpu.make_async_copy(r1.at[:15], r1.at[:15], sem1.at[0]).wait()

    @pl.when(jnp.logical_not(home))
    def _():
        pltpu.make_async_copy(r1.at[0], r1.at[0], sem1.at[0]).wait()

    total = z_sum(0)
    for i in range(2):
        t[i] = total[8 * i : 8 * i + 8]

    def band_copy(j, core):
        row = target(0, j)[1]
        chip = chip_at(2 * c + row, x)
        copy = pltpu.make_async_remote_copy(
            src_ref=t.at[row], dst_ref=r6.at[y], send_sem=sem6.at[0], recv_sem=sem6.at[1],
            device_id=(chip, core), device_id_type=MESH,
        )
        return copy, jnp.logical_and(chip == s, c == core)

    for j in range(2):
        for core in (1, 0):
            copy, mine = band_copy(j, core)
            if not j:
                copy.start()
            else:

                @pl.when(jnp.logical_not(mine))
                def _():
                    copy.start()

                @pl.when(mine)
                def _():
                    pltpu.make_async_copy(t.at[y % 2], r6.at[y], sem6.at[1]).start()

    total = z_sum(1)
    for i in range(4):
        q[i] = total[4 * i : 4 * i + 4]

    def out_copy(dx, core):
        cx = (x + dx) % 4
        copy = pltpu.make_async_remote_copy(
            src_ref=q.at[cx], dst_ref=r5.at[2 * x + c], send_sem=sem5.at[0], recv_sem=sem5.at[1],
            device_id=(chip_at(y, cx), core), device_id_type=MESH,
        )
        return copy, jnp.logical_and(dx == 0, c == core)

    for dx in (2, 1, 3, 0):
        for core in (1, 0):
            copy, mine = out_copy(dx, core)
            if dx:
                copy.start()
            else:

                @pl.when(jnp.logical_not(mine))
                def _():
                    copy.start()

                @pl.when(mine)
                def _():
                    pltpu.make_async_copy(q.at[x], r5.at[2 * x + c], sem5.at[1]).start()

    pltpu.make_async_copy(r3.at[1:], r3.at[1:], sem3.at[0]).wait()
    lane, rho = iota((8, 256), 1), iota((8, 256), 0)
    angle = (rho % 4) * (lane + 256 * c) + 128 * (rho // 4)
    turn_real, turn_imag = cos512(angle), cos512(angle - 128)
    side = jnp.where(rho < 4, -1.0, 1.0)

    pltpu.make_async_copy(r6, r6, sem6.at[1]).wait()
    halves = [jnp.concatenate((r6[2 * i], r6[2 * i + 1]), axis=1) for i in range(2)]
    sums = dot3(jnp.concatenate(halves, axis=0), e_high[...], e_low[...])
    sign = (1 - 2 * (lane % 2)).astype(F32)
    cosine = sums[:8, :256] + sign * sums[8:, :256]
    sine = sums[:8, 256:] + sign * sums[8:, 256:]
    result = cosine - side * jnp.concatenate((sine[4:], sine[:4]), axis=0)
    out[0] = result[:4]
    out[1] = result[4:]

    pltpu.make_async_copy(r5, r5, sem5.at[1]).wait()
    mask = iota((8, 128), 0) == iota((8, 128), 1) % 8
    columns = []
    for j in range(8):
        rows = r5[j]
        columns.append(jnp.concatenate([jnp.where(mask, rows[i : i + 1], 0.0) for i in range(4)], axis=0))
    moved = dot3(jnp.concatenate(columns, axis=1), back_high[...], back_low[...])
    reals, imags = [], []
    for i in range(4):
        tile = moved[8 * i : 8 * i + 8]
        sine = tile[:, 128:]
        pair = tile[:, :128] + side[:, :128] * jnp.concatenate((sine[4:], sine[:4]), axis=0)
        twice = jnp.concatenate((pair, pair), axis=1)
        reals.append(jnp.sum(twice * turn_real, axis=0, keepdims=True))
        imags.append(jnp.sum(twice * turn_imag, axis=0, keepdims=True))
    out[2] = jnp.concatenate(reals, axis=0)
    out[3] = jnp.concatenate(imags, axis=0)

    pltpu.make_async_copy(r5.at[:7], r5.at[:7], sem5.at[0]).wait()
    pltpu.make_async_copy(r6.at[:3], r6.at[:3], sem6.at[0]).wait()

    @pl.when(jnp.logical_not(home))
    def _():
        pltpu.make_async_copy(r6.at[0], r6.at[0], sem6.at[0]).wait()


def per_device(frames, aperture, upper_pixels, lower_pixels):
    tiled = frames.reshape(128, 4, 4, 128).transpose(0, 2, 1, 3).reshape(128, 2, 8, 128)
    operands = (tiled, aperture.reshape(1, 256), upper_pixels.T, lower_pixels.T)
    hbm = pl.BlockSpec(memory_space=pltpu.HBM)
    dma = pltpu.SemaphoreType.DMA
    both = pl.pallas_call(
        kernel,
        out_shape=pltpu.VMEM((4, 4, 256), F32),
        in_specs=[hbm] * 4,
        out_specs=pl.BlockSpec(memory_space=pltpu.VMEM),
        scratch_shapes=[
            pltpu.VMEM((128, 2, 8, 128), F32),
            pltpu.VMEM((1, 256), jnp.int32),
            pltpu.VMEM((64, 128), jnp.int32),
            pltpu.VMEM((64, 128), jnp.int32),
            pltpu.VMEM((128, 128), F32),
            pltpu.VMEM((2, 2, 4, 2, 4, 16, 128), F32),
            pltpu.VMEM((16, 4, 16, 128), F32),
            pltpu.VMEM((16, 4, 16, 128), F32),
            pltpu.VMEM((8, 32, 128), F32),
            pltpu.VMEM((8, 32, 128), F32),
            pltpu.VMEM((4, 4, 128), F32),
            pltpu.VMEM((8, 4, 128), F32),
            pltpu.VMEM((2, 8, 128), F32),
            pltpu.VMEM((4, 8, 128), F32),
            pltpu.VMEM((256, 512), BF16),
            pltpu.VMEM((256, 512), BF16),
            pltpu.VMEM((1024, 256), BF16),
            pltpu.VMEM((1024, 256), BF16),
            dma((3 + LOADS,)), dma((17,)), dma((2,)), dma((16,)), dma((2,)), dma((2,)),
        ],
        compiler_params=pltpu.CompilerParams(
            collective_id=0, has_side_effects=True, vmem_limit_bytes=32 * 1024 * 1024
        ),
    )(*[pltpu.with_memory_space_constraint(operand, pltpu.HBM) for operand in operands])
    return both[:2], both[2:].transpose(0, 2, 1)


def solution(mesh):
    placed = (P("det", "scan", None), P(), P(), P())
    return jax.shard_map(
        per_device,
        mesh=mesh,
        in_specs=placed,
        out_specs=(P(None, "scan", "det"), P(None, "det", "scan")),
        check_vma=False,
    )
```

```python
import math

import jax
import jax.numpy as jnp
from jax import lax
from jax.experimental import pallas as pl
from jax.experimental.pallas import tpu as pltpu
from jax.sharding import PartitionSpec as P

MESH = pl.DeviceIdType.MESH
F32 = jnp.float32
BF16 = jnp.bfloat16
UNIT = 2.0 * math.pi / 512
SIN = (-1.0 / 6, 1.0 / 120, -1.0 / 5040, 1.0 / 362880, -1.0 / 39916800)


def cos512(m):
    m = m & 511
    t = (128 - jnp.minimum(m, 512 - m)).astype(F32) * UNIT
    t2 = t * t
    poly = jnp.full_like(t, SIN[-1])
    for coefficient in SIN[-2::-1]:
        poly = poly * t2 + coefficient
    return t + t * (t2 * poly)


def split(a):
    high = a.astype(BF16)
    return high, (a - high.astype(F32)).astype(BF16)


def dot(a, b):
    return jnp.dot(a, b, preferred_element_type=F32)


def dot3(a, b_high, b_low):
    rows = a.shape[0]
    a_high, a_low = split(a)
    both = dot(jnp.concatenate((a_high, a_low), axis=0), b_high)
    return both[:rows] + both[rows:] + dot(a_high, b_low)


def iota(shape, dimension):
    return lax.broadcasted_iota(jnp.int32, shape, dimension)


LOADS = 4


def kernel(
    frames, aperture, upper, lower,
    out,
    f, ap, up, lo, w, a, b, r1, zs, r3, q, r5, t, r6, e_high, e_low, back_high, back_low,
    load_sem, swap_sem, sem1, sem3, sem5, sem6,
):
    s = lax.axis_index("scan")
    c = lax.axis_index("det")
    y, z, x = s // 32, (s // 4) % 8, s % 4
    me = y * 4 + x
    home = y // 2 == c

    def chip_at(cy, cx):
        return cy * 32 + z * 4 + cx

    first_row = jnp.where(home, 1 - y % 2, y % 2)
    TARGETS = [(dx, j, k) for k in range(2) for j in range(2) for dx in (2, 1, 3, 0)]

    def target(dx, j):
        return (x + dx) % 4, first_row * (1 - j) + (1 - first_row) * j

    def z_peer(d):
        return s + ((z + d) % 8 - z) * 4

    barrier = pltpu.get_barrier_semaphore()

    def greet(scan, det):
        pl.semaphore_signal(barrier, inc=1, device_id=(scan, det), device_id_type=MESH)

    for d in (4, 3, 5, 2, 6, 1, 7):
        greet(z_peer(d), c)
    for dx in (2, 1, 3, 0):
        for dy in (2, 1, 3, 0):
            if dx or dy:
                greet(chip_at((y + dy) % 4, (x + dx) % 4), y // 2)
        if dx:
            greet(chip_at(y, (x + dx) % 4), 1 - y // 2)
    greet(s, 1 - c)

    loads = [
        pltpu.make_async_copy(upper, up, load_sem.at[0]),
        pltpu.make_async_copy(lower, lo, load_sem.at[1]),
        pltpu.make_async_copy(aperture, ap, load_sem.at[2]),
    ]
    for i in range(LOADS):
        pixels = pl.ds(i * (128 // LOADS), 128 // LOADS)
        loads.append(pltpu.make_async_copy(frames.at[pixels], f.at[pixels], load_sem.at[3 + i]))
    for load in loads:
        load.start()

    for load in loads[:3]:
        load.wait()
    pixel = (iota((128, 128), 0) + 128 * c).astype(F32).astype(BF16)
    one, none = jnp.ones((128, 128), BF16), jnp.zeros((128, 128), BF16)

    def row_of(ref, j):
        return jnp.broadcast_to(ref[pl.ds(j, 1), :], (128, 128)).astype(F32).astype(BF16)

    def count(j, total):
        total = total + jnp.where(row_of(up, j) == pixel, one, none)
        return total - jnp.where(row_of(lo, j) == pixel, one, none)

    counts = lax.fori_loop(0, 64, count, none, unroll=4)
    w[...] = (counts.astype(F32) * (64**-0.5 / 512)).T
    tiles = [w[pl.ds(32 * (i % 4) + i // 4, 8, stride=4), :] for i in range(16)]
    inside = jnp.where(c == 0, ap[:, :128], ap[:, 128:]).astype(F32)
    weight = (jnp.concatenate(tiles, axis=0) * inside).astype(BF16)
    weight = jnp.concatenate((weight, weight), axis=1)

    flat = f.reshape(2048, 128)

    def weighted(half):
        for i in range(4):
            rows = [flat[pl.ds(8 * half + 4 * j + i, 128, stride=16), :] for j in range(2)]
            high, low = split(jnp.concatenate(rows, axis=1))
            sums = dot(weight, jnp.concatenate((high, low), axis=0))
            for j in range(2):
                a[half, j, :, :, i] = sums[:, 128 * j : 128 * j + 128].reshape(4, 2, 16, 128)

    for load in loads[3:]:
        load.wait()
    weighted(1 - c)
    weighted(c)

    pl.semaphore_wait(barrier, jnp.where(home, 22, 30))

    def swap_copy(i):
        dx, j, k = TARGETS[i]
        cx, row = target(dx, j)
        far_row = jnp.where(home, y % 2, 1 - y % 2) * (1 - j) + jnp.where(home, 1 - y % 2, y % 2) * j
        return pltpu.make_async_remote_copy(
            src_ref=a.at[1 - c, far_row, cx, (1 - c + k) % 2], dst_ref=b.at[i],
            send_sem=swap_sem.at[16], recv_sem=swap_sem.at[i], device_id=(s, 1 - c), device_id_type=MESH,
        )

    for i in range(16):
        swap_copy(i).start()

    def first_copy(i):
        dx, j, k = TARGETS[i]
        cx, row = target(dx, j)
        chip = chip_at(2 * c + row, cx)
        copy = pltpu.make_async_remote_copy(
            src_ref=b.at[i], dst_ref=r1.at[me], send_sem=sem1.at[0], recv_sem=sem1.at[1],
            device_id=(chip, (c + k) % 2), device_id_type=MESH,
        )
        return copy, chip == s

    for i, (dx, j, k) in enumerate(TARGETS):
        cx, row = target(dx, j)
        swap_copy(i).wait_recv()
        b[i] = b[i] + a[c, row, cx, (c + k) % 2]
        copy, mine = first_copy(i)
        if dx or k:
            copy.start()
        else:

            @pl.when(jnp.logical_not(mine))
            def _():
                copy.start()

            @pl.when(mine)
            def _():
                pltpu.make_async_copy(b.at[i], r1.at[me], sem1.at[1]).start()

    row, column = iota((64, 512), 0), iota((64, 512), 1)
    chip = (column // 128) * 32 + 4 * z + (column // 32) % 4
    place = 4 * chip + (column // 8) % 4
    same = row // 8 == column % 8
    lefts = []
    for i in range(2):
        block = (2 * c + i) * 32 + x + 4 * (row // 8)
        left = cos512((4 * block + row % 4) * place + 32 * (row % 8 - row % 4))
        lefts.append(split(jnp.where(same, left, 0.0)))

    frequency = iota((256, 512), 1)
    wide = frequency % 256 + 256 * c
    table_high, table_low = split(cos512(wide * iota((256, 512), 0) - 128 * (frequency // 256)))
    e_high[...] = table_high
    e_low[...] = table_low

    n, source = iota((1024, 256), 1), iota((1024, 256), 0)
    source_block = ((source // 64) % 4) * 32 + source // 256 + 4 * ((source // 8) % 8)
    table_high, table_low = split(cos512(4 * source_block * (n % 128) - 128 * (n // 128)))
    back_high[...] = table_high
    back_low[...] = table_low

    pltpu.make_async_copy(r1, r1, sem1.at[1]).wait()
    parts = []
    for i in range(2):
        right = jnp.concatenate([r1[k, :, 8 * i : 8 * i + 8].reshape(32, 128) for k in range(16)], axis=0)
        right_high, right_low = split(right)
        left_high, left_low = lefts[i]
        both = dot(jnp.concatenate((left_high, left_low), axis=0), right_high)
        parts.append((both[:64] + both[64:]) + dot(left_high, right_low))

    turned = jnp.concatenate(parts, axis=0).T
    for i in range(8):
        zs[i, :8] = parts[0][8 * i : 8 * i + 8]
        zs[i, 8:16] = parts[1][8 * i : 8 * i + 8]
        zs[i, 16:] = turned[16 * i : 16 * i + 16]

    def third_copy(d):
        return pltpu.make_async_remote_copy(
            src_ref=zs.at[(z + d) % 8], dst_ref=r3.at[d], send_sem=sem3.at[0], recv_sem=sem3.at[d],
            device_id=(z_peer(d), c), device_id_type=MESH,
        )

    for d in (4, 5, 3, 6, 2, 7, 1):
        third_copy(d).start()

    pltpu.make_async_copy(r1, r1, swap_sem.at[16]).wait()
    pltpu.make_async_copy(r1.at[:15], r1.at[:15], sem1.at[0]).wait()

    @pl.when(jnp.logical_not(home))
    def _():
        pltpu.make_async_copy(r1.at[0], r1.at[0], sem1.at[0]).wait()

    total = zs[z]
    for d in (1, 7, 2, 6, 3, 5, 4):
        third_copy(d).wait_recv()
        total = total + r3[d]
    for i in range(2):
        t[i] = total[8 * i : 8 * i + 8]

    def band_copy(j, core):
        row = target(0, j)[1]
        chip = chip_at(2 * c + row, x)
        copy = pltpu.make_async_remote_copy(
            src_ref=t.at[row], dst_ref=r6.at[y], send_sem=sem6.at[0], recv_sem=sem6.at[1],
            device_id=(chip, core), device_id_type=MESH,
        )
        return copy, jnp.logical_and(chip == s, c == core)

    for core in (1, 0):
        for j in range(2):
            copy, mine = band_copy(j, core)

            @pl.when(jnp.logical_not(mine))
            def _():
                copy.start()

            @pl.when(mine)
            def _():
                pltpu.make_async_copy(t.at[y % 2], r6.at[y], sem6.at[1]).start()

    for i in range(4):
        q[i] = total[16 + 4 * i : 20 + 4 * i]

    def out_copy(dx, core):
        cx = (x + dx) % 4
        copy = pltpu.make_async_remote_copy(
            src_ref=q.at[cx], dst_ref=r5.at[2 * x + c], send_sem=sem5.at[0], recv_sem=sem5.at[1],
            device_id=(chip_at(y, cx), core), device_id_type=MESH,
        )
        return copy, jnp.logical_and(dx == 0, c == core)

    for dx in (2, 1, 3, 0):
        for core in (1, 0):
            copy, mine = out_copy(dx, core)
            if dx:
                copy.start()
            else:

                @pl.when(jnp.logical_not(mine))
                def _():
                    copy.start()

                @pl.when(mine)
                def _():
                    pltpu.make_async_copy(q.at[x], r5.at[2 * x + c], sem5.at[1]).start()

    pltpu.make_async_copy(r3.at[1:], r3.at[1:], sem3.at[0]).wait()
    lane, rho = iota((8, 256), 1), iota((8, 256), 0)
    angle = (rho % 4) * (lane + 256 * c) + 128 * (rho // 4)
    turn_real, turn_imag = cos512(angle), cos512(angle - 128)
    side = jnp.where(rho < 4, -1.0, 1.0)

    pltpu.make_async_copy(r5, r5, sem5.at[1]).wait()
    mask = iota((8, 128), 0) == iota((8, 128), 1) % 8
    columns = []
    for j in range(8):
        rows = r5[j]
        columns.append(jnp.concatenate([jnp.where(mask, rows[i : i + 1], 0.0) for i in range(4)], axis=0))
    moved = dot3(jnp.concatenate(columns, axis=1), back_high[...], back_low[...])
    reals, imags = [], []
    for i in range(4):
        tile = moved[8 * i : 8 * i + 8]
        sine = tile[:, 128:]
        pair = tile[:, :128] + side[:, :128] * jnp.concatenate((sine[4:], sine[:4]), axis=0)
        twice = jnp.concatenate((pair, pair), axis=1)
        reals.append(jnp.sum(twice * turn_real, axis=0, keepdims=True))
        imags.append(jnp.sum(twice * turn_imag, axis=0, keepdims=True))
    out[2] = jnp.concatenate(reals, axis=0)
    out[3] = jnp.concatenate(imags, axis=0)

    pltpu.make_async_copy(r6, r6, sem6.at[1]).wait()
    halves = [jnp.concatenate((r6[2 * i], r6[2 * i + 1]), axis=1) for i in range(2)]
    sums = dot3(jnp.concatenate(halves, axis=0), e_high[...], e_low[...])
    sign = (1 - 2 * (lane % 2)).astype(F32)
    cosine = sums[:8, :256] + sign * sums[8:, :256]
    sine = sums[:8, 256:] + sign * sums[8:, 256:]
    result = cosine - side * jnp.concatenate((sine[4:], sine[:4]), axis=0)
    out[0] = result[:4]
    out[1] = result[4:]

    pltpu.make_async_copy(r5.at[:7], r5.at[:7], sem5.at[0]).wait()
    pltpu.make_async_copy(r6.at[:3], r6.at[:3], sem6.at[0]).wait()

    @pl.when(jnp.logical_not(home))
    def _():
        pltpu.make_async_copy(r6.at[0], r6.at[0], sem6.at[0]).wait()


def per_device(frames, aperture, upper_pixels, lower_pixels):
    tiled = frames.reshape(128, 4, 4, 128).transpose(0, 2, 1, 3).reshape(128, 2, 8, 128)
    operands = (tiled, aperture.reshape(1, 256), upper_pixels.T, lower_pixels.T)
    hbm = pl.BlockSpec(memory_space=pltpu.HBM)
    dma = pltpu.SemaphoreType.DMA
    both = pl.pallas_call(
        kernel,
        out_shape=pltpu.VMEM((4, 4, 256), F32),
        in_specs=[hbm] * 4,
        out_specs=pl.BlockSpec(memory_space=pltpu.VMEM),
        scratch_shapes=[
            pltpu.VMEM((128, 2, 8, 128), F32),
            pltpu.VMEM((1, 256), jnp.int32),
            pltpu.VMEM((64, 128), jnp.int32),
            pltpu.VMEM((64, 128), jnp.int32),
            pltpu.VMEM((128, 128), F32),
            pltpu.VMEM((2, 2, 4, 2, 4, 16, 128), F32),
            pltpu.VMEM((16, 4, 16, 128), F32),
            pltpu.VMEM((16, 4, 16, 128), F32),
            pltpu.VMEM((8, 32, 128), F32),
            pltpu.VMEM((8, 32, 128), F32),
            pltpu.VMEM((4, 4, 128), F32),
            pltpu.VMEM((8, 4, 128), F32),
            pltpu.VMEM((2, 8, 128), F32),
            pltpu.VMEM((4, 8, 128), F32),
            pltpu.VMEM((256, 512), BF16),
            pltpu.VMEM((256, 512), BF16),
            pltpu.VMEM((1024, 256), BF16),
            pltpu.VMEM((1024, 256), BF16),
            dma((3 + LOADS,)), dma((17,)), dma((2,)), dma((8,)), dma((2,)), dma((2,)),
        ],
        compiler_params=pltpu.CompilerParams(
            collective_id=0, has_side_effects=True, vmem_limit_bytes=32 * 1024 * 1024
        ),
    )(*[pltpu.with_memory_space_constraint(operand, pltpu.HBM) for operand in operands])
    return both[:2], both[2:].transpose(0, 2, 1)


def solution(mesh):
    placed = (P("det", "scan", None), P(), P(), P())
    return jax.shard_map(
        per_device,
        mesh=mesh,
        in_specs=placed,
        out_specs=(P(None, "scan", "det"), P(None, "det", "scan")),
        check_vma=False,
    )
```
